128 devices in a mesh: xs: 16 (over y, x), ls: 8 (over z, core).
Axes of the slice: x: 4, y: 4, z: 4, core: 2. Of those that a mesh axis runs over, the one named last changes fastest.
Arguments:
- position: float32 [3, 1048576], P(None, ('xs', 'ls')), may hold values from -6 to 6
- velocity: float32 [3, 1048576], P(None, ('xs', 'ls')), may hold values from -6 to 6
- radius: float32 [1048576], P(('xs', 'ls')), may hold values from 0.3 to 0.6
- partners: int32 [8, 1048576], P(None, ('xs', 'ls')), may hold values from 0 to 255
- owner: int32 [1048576, 1], P(('xs', 'ls')), may hold values from 0 to 127; in each aligned block of 8192 rows (0 to 8191, 8192 to 16383, ...) at most 128 rows name the same one
- cell: int32 [1048576], P(('xs', 'ls')), may hold values from 0 to 16383
- fluid: float32 [3, 128, 64, 256], P(None, 'xs', 'ls'), may hold values from -6 to 6
Outputs:
- grain_velocity: float32 [3, 1048576], P(None, ('xs', 'ls'))
- fluid_star: float32 [3, 128, 64, 256], P(None, 'xs', 'ls')
The draws below stay inside these ranges and needn't reach their ends.
Inputs may be any that keep to these rules, and one draw needn't show every extreme that they name: Among the 8192 grains of one device at most 128 name the same owner, a bound that some block reaches of them.
All inputs are finite; a program needn't handle non-finite values.
Results may differ from the reference program's by a relative error of at most 0.0003.
Values sent between devices are 32-bit elements; how exact they have to be, the bound alone decides.
A program may use at most 192 MiB of HBM per device.

```python
import math
import jax
import jax.numpy as jnp
import numpy as np
from jax import lax

BLOCK = 128
KC = 8
GDEV = 8192
CX = 8
CY = 8
CZ = 256
CELLS = 16384
MOST = 128
NG = 1048576
NX = 128
NY = 64
NZ = 256
DEVICES = 128


def touch_ends(result, own_key, low, high):
    longest = result.shape.index(max(result.shape))
    spots = []
    for shift in (0, 1):
        where = [jax.random.randint(jax.random.fold_in(own_key, axis), (), 0, length) for axis, length in enumerate(result.shape)]
        where[longest] = (where[longest] + shift) % result.shape[longest]
        spots.append(tuple(where))
    return result.at[spots[0]].set(low).at[spots[1]].set(high)


def level_of(rng, shape, pieces, least, largest):
    level = 1.0
    for axis_at, blocks in pieces:
        steps = jax.random.uniform(jax.random.fold_in(jax.random.fold_in(rng, 6), axis_at), (blocks,), jnp.float32, least / len(pieces), largest / len(pieces))
        level = level * jnp.repeat(jnp.exp(steps), shape[axis_at] // blocks).reshape((-1,) + (1,) * (len(shape) - 1 - axis_at))
    return level


def assign_block(own_key, own, number, rows, number_of, top, most, skew):
    order = jax.random.permutation(own_key, number_of)
    packed, usual = load_shares(number_of, rows * top, most, skew, True), load_shares(number_of, rows * top, most, skew, False)
    places = jnp.arange(number_of)

    def named(tallies, turn):
        used = int((tallies > 0).sum())
        fixed = max(1, used // 4)
        shifted = fixed + (places - fixed + turn * (used - fixed)) % max(1, number_of - fixed)
        return jnp.zeros((number_of,), jnp.int32).at[order[jnp.where(places < fixed, places, shifted)]].set(jnp.asarray(tallies, jnp.int32))

    tallies = jnp.where(number % 4 == 0, named(packed, number // 4), named(usual, number - number // 4 - 1))
    mixed = jax.random.permutation(jax.random.fold_in(own, 3), number_of)
    donor, receiver = mixed[0:number_of // 2 * 2:2], mixed[1:number_of // 2 * 2:2]
    margin = jnp.minimum(tallies[donor] - 1, most - tallies[receiver]) // 2
    margin = jnp.where((donor == order[0]) | (receiver == order[0]) | (tallies[receiver] == 0), 0, jnp.maximum(margin, 0))
    shifted = jax.random.randint(jax.random.fold_in(own, 4), (number_of // 2,), 0, 1 << 20) % (margin + 1)
    tallies = tallies.at[donor].add(-shifted).at[receiver].add(shifted)
    labels = jnp.searchsorted(jnp.cumsum(tallies), jnp.arange(rows * top), side="right").astype(jnp.int32)
    listing = labels.reshape(top, rows).T
    listing = listing[jax.random.permutation(jax.random.fold_in(own, 1), rows)]
    turn = jax.random.randint(jax.random.fold_in(own, 2), (rows, 1), 0, top)
    return jnp.take_along_axis(listing, (jnp.arange(top)[None, :] + turn) % top, axis=1)


def load_shares(amount, total, most, skew, full):
    weights = [(1 << 20) // math.isqrt(rank ** skew) + 1 for rank in range(1, amount + 1)]
    largest = most if full else min(most, max(-(-total // amount), total * weights[0] // sum(weights)))
    least = 1 if total - largest >= amount - 1 else 0
    holding, spare = [largest] + [least] * (amount - 1), total - largest - least * (amount - 1)
    while spare > 0:
        candidates = [i for i in range(1, amount) if holding[i] < largest] or [i for i in range(1, amount) if holding[i] < most]
        mass, remaining = sum([weights[i] for i in candidates]), spare
        for i in candidates:
            more = min(most - holding[i], max(1, remaining * weights[i] // mass), spare)
            holding[i] = holding[i] + more
            spare = spare - more
    return np.array(holding)


def bell_draw(key, dims, scale, most, pieces=(), kind=jnp.bfloat16):
    loudness = level_of(key, dims, pieces, -0.22, 0.18) if pieces else 1.0
    values = jax.random.normal(key, dims, jnp.float32) * scale * loudness
    return jnp.minimum(jnp.maximum(values, -most), most).astype(kind)


def setup_inputs(seed: int = 0) -> dict:
    arg_keys = jax.random.split(jax.random.key(seed), 8)
    position = bell_draw(arg_keys[0], (3, NG), 0.4, 6.0, ((1, 128),), jnp.float32)
    velocity = bell_draw(arg_keys[1], (3, NG), 1.0, 6.0, ((1, 128),), jnp.float32)
    radius = jnp.clip(0.3 + 0.3 * jax.random.uniform(arg_keys[2], (NG,), jnp.float32) ** level_of(arg_keys[2], (NG,), ((0, 128),), -0.2, 0.2), 0.3, 0.6)
    partners = touch_ends(jax.random.randint(arg_keys[3], (KC, NG), 0, 2 * BLOCK), jax.random.fold_in(arg_keys[3], 1), 0, (2 * BLOCK) - 1).astype(jnp.int32)
    owner_keys = jax.random.split(jax.random.fold_in(arg_keys[4], 1), NG // GDEV)
    owner_turns = jax.random.permutation(jax.random.fold_in(arg_keys[4], 3), NG // GDEV)
    owner = jax.vmap(lambda own, number: assign_block(jax.random.fold_in(arg_keys[4], 2), own, number, GDEV, DEVICES, 1, MOST, 2))(owner_keys, owner_turns).reshape((NG, 1))
    cell = touch_ends(jax.random.randint(arg_keys[5], (NG,), 0, CELLS), jax.random.fold_in(arg_keys[5], 1), 0, CELLS - 1).astype(jnp.int32)
    fluid = bell_draw(arg_keys[6], (3, NX, NY, NZ), 1.0, 6.0, ((1, 16), (2, 8)), jnp.float32)
    return {"position": position, "velocity": velocity, "radius": radius, "partners": partners, "owner": owner, "cell": cell, "fluid": fluid}


def contact_force(position, radius, ghost_pos, ghost_rad, partners):
    count = radius.shape[0]
    blocks = count // BLOCK
    own = jnp.concatenate([position, radius[None]], axis=0).reshape(4, blocks, BLOCK)
    other = jnp.concatenate([ghost_pos, ghost_rad[None]], axis=0).reshape(4, blocks, BLOCK)
    window = jnp.concatenate([own, other], axis=2).reshape(4, blocks * 2 * BLOCK)
    offset = (jnp.arange(blocks, dtype=jnp.int32) * (2 * BLOCK))[None, :, None]
    flat = (partners.reshape(KC, blocks, BLOCK).astype(jnp.int32) + offset).reshape(-1)
    picked = window[:, flat].reshape(4, KC, blocks, BLOCK)
    diff = position.reshape(3, 1, blocks, BLOCK) - picked[0:3]
    dist = jnp.sqrt(lax.optimization_barrier(jnp.sum(diff * diff, axis=0)))
    delta = jnp.maximum(radius.reshape(1, blocks, BLOCK) + picked[3] - dist, 0.0)
    scale = 10.0 * delta * jnp.sqrt(delta) / jnp.maximum(dist, 0.1)
    return lax.optimization_barrier(jnp.sum(scale[None] * diff, axis=1)).reshape(3, count)

def reference(position, velocity, radius, partners, owner, cell, fluid):
    n_xs = NX // CX
    n_ls = NY // CY
    devices = n_xs * n_ls
    pos_dev = position.reshape(3, n_xs, n_ls, GDEV)
    rad_dev = radius.reshape(n_xs, n_ls, GDEV)
    ghost_pos = jnp.roll(pos_dev, 1, axis=2).reshape(3, devices, GDEV).transpose(1, 0, 2)
    ghost_rad = jnp.roll(rad_dev, 1, axis=1).reshape(devices, GDEV)
    own_pos = position.reshape(3, devices, GDEV).transpose(1, 0, 2)
    own_rad = radius.reshape(devices, GDEV)
    own_par = partners.reshape(KC, devices, GDEV).transpose(1, 0, 2)
    contact = lax.map(lambda a: contact_force(a[0], a[1], a[2], a[3], a[4]), (own_pos, own_rad, ghost_pos, ghost_rad, own_par))
    contact = contact.transpose(1, 0, 2).reshape(3, NG)
    beta = 2.0 * radius
    volume = 4.0 / 3.0 * math.pi * radius * radius * radius
    terms = jnp.concatenate([beta[None] * velocity, beta[None], volume[None]], axis=0)
    gid = owner[:, 0].astype(jnp.int32) * CELLS + cell
    sums = jax.ops.segment_sum(terms.T, gid, num_segments=devices * CELLS)
    grid = sums.T.reshape(5, n_xs, n_ls, CX, CY, CZ).transpose(0, 1, 3, 2, 4, 5).reshape(5, NX, NY, NZ)
    drag_momentum = grid[0:3]
    drag_sum = grid[3]
    solid = grid[4]
    beside = jnp.roll(fluid, 1, axis=1) + jnp.roll(fluid, -1, axis=1)
    beside = beside + jnp.roll(fluid, 1, axis=2) + jnp.roll(fluid, -1, axis=2)
    padded = jnp.pad(fluid, ((0, 0), (0, 0), (0, 0), (1, 1)))
    beside = beside + padded[:, :, :, 2:] + padded[:, :, :, :-2]
    lap = beside - 6.0 * fluid
    porosity = 1.0 / (1.0 + solid)
    fluid_star = (porosity[None] * fluid + 0.1 * lap + 0.1 * drag_momentum) / (porosity + 0.1 * drag_sum)[None]
    flat = fluid_star.reshape(3, n_xs, CX, n_ls, CY, CZ).transpose(0, 1, 3, 2, 4, 5).reshape(3, devices * CELLS)
    seen = flat[:, gid]
    grain_velocity = velocity + 0.1 * (contact + beta[None] * (seen - velocity)) / (2.65 * volume)[None]
    return (grain_velocity, fluid_star)
```

```python
import math

import jax
import jax.numpy as jnp
from jax import lax
from jax.experimental import pallas as pl
from jax.experimental.pallas import tpu as pltpu
from jax.sharding import PartitionSpec as P

F32 = jnp.float32
BF16 = jnp.bfloat16
SLOTS = 128
ROWS = 64
WIDE = 256
NT = (((1,), (1,)), ((), ()))
NN = (((1,), (0,)), ((), ()))


def halves(x):
    high = x.astype(BF16)
    return high, (x - high.astype(F32)).astype(BF16)


def dot(a, b, dims):
    return lax.dot_general(a, b, dims, preferred_element_type=F32)


def spread(row, high, iota):
    return jnp.where(iota == high, row, jnp.zeros((), BF16))


def place_kernel(owner_ref, cell_ref, velocity_ref, radius_ref, send_ref, slot_ref, acc_ref):
    count = owner_ref.shape[1]
    chunk = 256
    owners = 2 * ROWS
    before = lax.broadcasted_iota(jnp.int32, (chunk, chunk), 0) <= lax.broadcasted_iota(
        jnp.int32, (chunk, chunk), 1
    )
    upper = jnp.where(before, 1.0, 0.0).astype(BF16)
    owner_iota = lax.broadcasted_iota(jnp.int32, (owners, chunk), 0)

    def rank(c, base):
        at = pl.ds(pl.multiple_of(c * chunk, chunk), chunk)
        mine = owner_iota == owner_ref[:, at]
        upto = dot(jnp.where(mine, 1.0, 0.0).astype(BF16), upper, NN) + base
        slot = jnp.sum(jnp.where(mine, upto, 0.0), axis=0, keepdims=True)
        slot_ref[:, at] = slot.astype(jnp.int32) - 1
        return upto[:, chunk - 1 :]

    lax.fori_loop(0, count // chunk, rank, jnp.zeros((owners, 1), F32), unroll=4)

    step = 512
    row_iota = lax.broadcasted_iota(jnp.int32, (ROWS, step), 0).astype(F32).astype(BF16)
    col_iota = lax.broadcasted_iota(jnp.int32, (WIDE, step), 0).astype(F32).astype(BF16)
    acc_ref[...] = jnp.zeros_like(acc_ref)

    def place(c, carry):
        at = pl.ds(pl.multiple_of(c * step, step), step)
        owner = owner_ref[:, at]
        low = (slot_ref[:, at] + (owner // ROWS) * SLOTS).astype(F32).astype(BF16)
        high = (owner % ROWS).astype(F32).astype(BF16)
        cell = cell_ref[:, at]
        parts = []
        for i in range(3):
            parts += halves(velocity_ref[i : i + 1, at])
        parts += halves(radius_ref[:, at])
        parts += [(cell // WIDE).astype(F32).astype(BF16), (cell % WIDE).astype(F32).astype(BF16)]
        mine = row_iota == high
        a = jnp.concatenate([jnp.where(mine, p, jnp.zeros((), BF16)) for p in parts], axis=0)
        b = jnp.where(col_iota == low, jnp.ones((), BF16), jnp.zeros((), BF16))
        acc_ref[...] += dot(a, b, NT)
        return carry

    lax.fori_loop(0, count // step, place, 0)
    for f in range(5):
        first = acc_ref[2 * f * ROWS : (2 * f + 1) * ROWS, :]
        second = acc_ref[(2 * f + 1) * ROWS : (2 * f + 2) * ROWS, :]
        value = first + second if f < 4 else first * float(WIDE) + second
        send_ref[0:ROWS, f, :] = value[:, :SLOTS]
        send_ref[ROWS:, f, :] = value[:, SLOTS:]


def star_kernel(got_ref, fluid_ref, xb_ref, xa_ref, yb_ref, ya_ref, star_ref, answer_ref, acc_ref, table_ref):
    cx, cy, cz = fluid_ref.shape[1:]
    sources = got_ref.shape[0]
    step = 512
    per = step // SLOTS
    row_iota = lax.broadcasted_iota(jnp.int32, (ROWS, step), 0).astype(F32).astype(BF16)
    col_iota = lax.broadcasted_iota(jnp.int32, (WIDE, step), 0).astype(F32).astype(BF16)
    one, zero = jnp.ones((), BF16), jnp.zeros((), BF16)
    acc_ref[...] = jnp.zeros_like(acc_ref)

    def cells(c):
        cell = jnp.concatenate([got_ref[c * per + i, 4:5, :] for i in range(per)], axis=1)
        high = jnp.floor(cell * (1.0 / WIDE))
        return high.astype(BF16), (cell - high * WIDE).astype(BF16)

    def add(c, carry):
        high, low = cells(c)
        rows = [
            jnp.concatenate([got_ref[c * per + i, f : f + 1, :] for i in range(per)], axis=1) for f in range(4)
        ]
        beta = 2.0 * rows[3]
        volume = 4.0 / 3.0 * math.pi * rows[3] * rows[3] * rows[3]
        parts = []
        for x in (beta * rows[0], beta * rows[1], beta * rows[2], beta, volume):
            parts += halves(x)
        mine = row_iota == high
        a = jnp.concatenate([jnp.where(mine, p, zero) for p in parts], axis=0)
        b = jnp.where(col_iota == low, one, zero)
        acc_ref[...] += dot(a, b, NT)
        return carry

    lax.fori_loop(0, sources // per, add, 0)

    def total(f):
        both = acc_ref[2 * f * ROWS : (2 * f + 1) * ROWS, :] + acc_ref[(2 * f + 1) * ROWS : (2 * f + 2) * ROWS, :]
        return both.reshape(cx, cy, cz)

    porosity = 1.0 / (1.0 + total(4))
    below = porosity + 0.1 * total(3)
    row = lax.broadcasted_iota(jnp.int32, (cx, cy, cz), 1)
    lane = lax.broadcasted_iota(jnp.int32, (cx, cy, cz), 2)
    for i in range(3):
        u = fluid_ref[i]
        beside = jnp.concatenate([u[1:], xa_ref[i]], axis=0) + jnp.concatenate([xb_ref[i], u[:-1]], axis=0)
        after = jnp.broadcast_to(ya_ref[i], (cx, cy, cz))
        before = jnp.broadcast_to(yb_ref[i], (cx, cy, cz))
        beside = beside + jnp.where(row == cy - 1, after, pltpu.roll(u, cy - 1, 1))
        beside = beside + jnp.where(row == 0, before, pltpu.roll(u, 1, 1))
        beside = beside + jnp.where(lane == cz - 1, 0.0, pltpu.roll(u, cz - 1, 2))
        beside = beside + jnp.where(lane == 0, 0.0, pltpu.roll(u, 1, 2))
        lap = beside - 6.0 * u
        star = (porosity * u + 0.1 * lap + 0.1 * total(i)) / below
        star_ref[i] = star
        high, low = halves(star.reshape(ROWS, WIDE))
        table_ref[i * ROWS : (i + 1) * ROWS, :] = high
        table_ref[(3 + i) * ROWS : (4 + i) * ROWS, :] = low

    row_f32 = lax.broadcasted_iota(jnp.int32, (ROWS, step), 0).astype(F32)

    def look(c, carry):
        high, low = cells(c)
        b = jnp.where(col_iota == low, one, zero)
        x = dot(table_ref[...], b, NN)
        mine = row_f32 == high.astype(F32)
        for i in range(3):
            both = x[i * ROWS : (i + 1) * ROWS] + x[(3 + i) * ROWS : (4 + i) * ROWS]
            picked = jnp.sum(jnp.where(mine, both, 0.0), axis=0, keepdims=True)
            for k in range(per):
                answer_ref[c * per + k, i : i + 1, :] = picked[:, k * SLOTS : (k + 1) * SLOTS]
        return carry

    lax.fori_loop(0, sources // per, look, 0)


def grain_kernel(
    back_ref, owner_ref, slot_ref, velocity_ref, radius_ref, position_ref, ghost_ref, ghost_radius_ref,
    partners_ref, out_ref, table_ref, contact_ref,
):
    count = owner_ref.shape[1]
    kc = partners_ref.shape[0]
    block = 128
    for i in range(3):
        both = jnp.concatenate([back_ref[0:ROWS, i, :], back_ref[ROWS:, i, :]], axis=1)
        high, low = halves(both)
        table_ref[i * ROWS : (i + 1) * ROWS, :] = high
        table_ref[(3 + i) * ROWS : (4 + i) * ROWS, :] = low

    def touch(c, carry):
        at = pl.ds(pl.multiple_of(c * block, block), block)
        index = partners_ref[:, at]
        ghost = index >= block
        local = jnp.where(ghost, index - block, index)

        def pick(own, other):
            a = jnp.take_along_axis(jnp.broadcast_to(own, (kc, block)), local, axis=1, mode="promise_in_bounds")
            b = jnp.take_along_axis(jnp.broadcast_to(other, (kc, block)), local, axis=1, mode="promise_in_bounds")
            return jnp.where(ghost, b, a)

        diff = [
            position_ref[i : i + 1, at] - pick(position_ref[i : i + 1, at], ghost_ref[i : i + 1, at]) for i in range(3)
        ]
        other = pick(radius_ref[:, at], ghost_radius_ref[:, at])
        dist = jnp.sqrt(diff[0] * diff[0] + diff[1] * diff[1] + diff[2] * diff[2])
        delta = jnp.maximum(radius_ref[:, at] + other - dist, 0.0)
        scale = 10.0 * delta * jnp.sqrt(delta) / jnp.maximum(dist, 0.1)
        for i in range(3):
            contact_ref[i : i + 1, at] = jnp.sum(scale * diff[i], axis=0, keepdims=True)
        return carry

    lax.fori_loop(0, count // block, touch, 0, unroll=4)

    step = 512
    col_iota = lax.broadcasted_iota(jnp.int32, (WIDE, step), 0).astype(F32).astype(BF16)
    row_iota = lax.broadcasted_iota(jnp.int32, (ROWS, step), 0)
    one, zero = jnp.ones((), BF16), jnp.zeros((), BF16)

    def finish(c, carry):
        at = pl.ds(pl.multiple_of(c * step, step), step)
        owner = owner_ref[:, at]
        low = (slot_ref[:, at] + (owner // ROWS) * SLOTS).astype(F32).astype(BF16)
        b = jnp.where(col_iota == low, one, zero)
        x = dot(table_ref[...], b, NN)
        mine = row_iota == owner % ROWS
        radius = radius_ref[:, at]
        beta = 2.0 * radius
        volume = 4.0 / 3.0 * math.pi * radius * radius * radius
        for i in range(3):
            both = x[i * ROWS : (i + 1) * ROWS] + x[(3 + i) * ROWS : (4 + i) * ROWS]
            seen = jnp.sum(jnp.where(mine, both, 0.0), axis=0, keepdims=True)
            velocity = velocity_ref[i : i + 1, at]
            out_ref[i : i + 1, at] = velocity + 0.1 * (
                contact_ref[i : i + 1, at] + beta * (seen - velocity)
            ) / (2.65 * volume)
        return carry

    lax.fori_loop(0, count // step, finish, 0)


def shifted(value, axis, steps):
    count = lax.axis_size(axis)
    return lax.ppermute(value, axis, [(source, (source + steps) % count) for source in range(count)])


def params():
    return pltpu.CompilerParams(vmem_limit_bytes=48 * 1024 * 1024)


def whole(n):
    return [pl.BlockSpec(memory_space=pltpu.VMEM)] * n


def shards(position, velocity, radius, partners, owner, cell, fluid):
    count = radius.shape[0]
    devices = lax.axis_size("xs") * lax.axis_size("ls")
    cx, cy, cz = fluid.shape[1:]
    radius = radius.reshape(1, count)
    owner = owner.reshape(1, count)
    cell = cell.reshape(1, count)
    ghost = shifted(position, "ls", 1)
    ghost_radius = shifted(radius, "ls", 1)
    x_before = shifted(fluid[:, cx - 1 :], "xs", 1)
    x_after = shifted(fluid[:, :1], "xs", -1)
    y_before = shifted(fluid[:, :, cy - 1 :], "ls", 1)
    y_after = shifted(fluid[:, :, :1], "ls", -1)
    send, slot = pl.pallas_call(
        place_kernel,
        out_shape=(
            jax.ShapeDtypeStruct((devices, 5, SLOTS), F32),
            jax.ShapeDtypeStruct((1, count), jnp.int32),
        ),
        in_specs=whole(4),
        out_specs=tuple(whole(2)),
        scratch_shapes=[pltpu.VMEM((10 * ROWS, WIDE), F32)],
        compiler_params=params(),
        cost_estimate=pl.CostEstimate(flops=3500000000, bytes_accessed=1000000, transcendentals=0),
        name="place",
    )(owner, cell, velocity, radius)
    got = lax.all_to_all(send, ("xs", "ls"), split_axis=0, concat_axis=0, tiled=True)
    star, answer = pl.pallas_call(
        star_kernel,
        out_shape=(
            jax.ShapeDtypeStruct(fluid.shape, F32),
            jax.ShapeDtypeStruct((devices, 3, SLOTS), F32),
        ),
        in_specs=whole(6),
        out_specs=tuple(whole(2)),
        scratch_shapes=[pltpu.VMEM((10 * ROWS, WIDE), F32), pltpu.VMEM((6 * ROWS, WIDE), BF16)],
        compiler_params=params(),
        cost_estimate=pl.CostEstimate(flops=9000000000, bytes_accessed=2000000, transcendentals=0),
        name="star",
    )(got, fluid, x_before, x_after, y_before, y_after)
    back = lax.all_to_all(answer, ("xs", "ls"), split_axis=0, concat_axis=0, tiled=True)
    grain_velocity = pl.pallas_call(
        grain_kernel,
        out_shape=jax.ShapeDtypeStruct(velocity.shape, F32),
        in_specs=whole(9),
        out_specs=pl.BlockSpec(memory_space=pltpu.VMEM),
        scratch_shapes=[pltpu.VMEM((6 * ROWS, WIDE), BF16), pltpu.VMEM(velocity.shape, F32)],
        compiler_params=params(),
        cost_estimate=pl.CostEstimate(flops=2000000000, bytes_accessed=1000000, transcendentals=0),
        name="grain",
    )(back, owner, slot, velocity, radius, position, ghost, ghost_radius, partners)
    return (grain_velocity, star)


def solution(mesh):
    placed = (
        P(None, ("xs", "ls")),
        P(None, ("xs", "ls")),
        P(("xs", "ls")),
        P(None, ("xs", "ls")),
        P(("xs", "ls"), None),
        P(("xs", "ls")),
        P(None, "xs", "ls", None),
    )
    return jax.shard_map(
        shards,
        mesh=mesh,
        in_specs=placed,
        out_specs=(P(None, ("xs", "ls")), P(None, "xs", "ls", None)),
        check_vma=False,
    )
```

```python
import functools
import math

import jax
import jax.numpy as jnp
from jax import lax
from jax.experimental import pallas as pl
from jax.experimental.pallas import tpu as pltpu
from jax.sharding import PartitionSpec as P

F32 = jnp.float32
BF16 = jnp.bfloat16
MESH = pl.DeviceIdType.MESH
SLOTS = 128
ROWS = 64
WIDE = 256
BLOCK = 128
STEP = 512
NT = (((1,), (1,)), ((), ()))
NN = (((1,), (0,)), ((), ()))


def halves(x):
    high = x.astype(BF16)
    return high, (x - high.astype(F32)).astype(BF16)


def dot(a, b, dims):
    return lax.dot_general(a, b, dims, preferred_element_type=F32)


def small_iota(rows, columns):
    return lax.broadcasted_iota(jnp.int32, (rows, columns), 0).astype(F32).astype(BF16)


def masked(mine, parts):
    return jnp.concatenate([jnp.where(mine, p, jnp.zeros((), BF16)) for p in parts], axis=0)


def marks(mine):
    return jnp.where(mine, jnp.ones((), BF16), jnp.zeros((), BF16))


def chunk_at(c, size):
    return pl.ds(pl.multiple_of(c * size, size), size)


def step_kernel(
    n_xs, n_ls,
    owner_in, cell_in, velocity_in, radius_in, position_in, partners_in, fluid_in,
    out_ref, star_ref,
    owner_ref, cell_ref, velocity_ref, radius_ref, position_ref, partners_ref, fluid_ref,
    slot_ref, acc_ref, table_ref, contact_ref, lap_ref,
    send_ref, got_ref, answer_ref, back_ref,
    ghost_ref, ghost_radius_ref, x_before_ref, x_after_ref, y_out_ref, y_before_ref, y_after_ref,
    in_sem, near_send, near_recv, out_sem, got_sem, answer_sem, back_sem,
):
    i = lax.axis_index("xs")
    j = lax.axis_index("ls")
    peers = n_xs * n_ls
    me = j * n_xs + i
    count = owner_ref.shape[1]

    barrier = pltpu.get_barrier_semaphore()

    def peer(k):
        return (i + k % n_xs) % n_xs, (j + k // n_xs) % n_ls

    arrivals = [
        pltpu.make_async_copy(source, target, in_sem.at[n])
        for n, (source, target) in enumerate(
            (
                (owner_in, owner_ref), (cell_in, cell_ref), (velocity_in, velocity_ref), (radius_in, radius_ref),
                (position_in, position_ref), (partners_in, partners_ref), (fluid_in, fluid_ref),
            )
        )
    ]
    for copy in arrivals:
        copy.start()

    def greet(k, carry):
        pl.semaphore_signal(barrier, inc=1, device_id=peer(k), device_id_type=MESH)
        return carry

    lax.fori_loop(1, peers, greet, 0)
    for copy in arrivals[:4]:
        copy.wait()

    def slot_row(owner):
        return (owner % n_ls) * n_xs + owner // n_ls

    rank_step = 256
    upper = jnp.where(
        lax.broadcasted_iota(jnp.int32, (rank_step, rank_step), 0)
        <= lax.broadcasted_iota(jnp.int32, (rank_step, rank_step), 1),
        1.0, 0.0,
    ).astype(BF16)
    owner_iota = lax.broadcasted_iota(jnp.int32, (peers, rank_step), 0)

    def rank(c, base):
        at = chunk_at(c, rank_step)
        mine = owner_iota == owner_ref[:, at]
        upto = dot(jnp.where(mine, 1.0, 0.0).astype(BF16), upper, NN) + base
        slot = jnp.sum(jnp.where(mine, upto, 0.0), axis=0, keepdims=True)
        slot_ref[:, at] = slot.astype(jnp.int32) - 1
        return upto[:, rank_step - 1 :]

    lax.fori_loop(0, count // rank_step, rank, jnp.zeros((peers, 1), F32), unroll=4)

    row_iota = small_iota(ROWS, STEP)
    col_iota = small_iota(WIDE, STEP)
    acc_ref[...] = jnp.zeros_like(acc_ref)

    def spot(at):
        row = slot_row(owner_ref[:, at])
        return row % ROWS, slot_ref[:, at] + (row // ROWS) * SLOTS

    def place(c, carry):
        at = chunk_at(c, STEP)
        high, low = spot(at)
        cell = cell_ref[:, at]
        parts = []
        for n in range(3):
            parts += halves(velocity_ref[n : n + 1, at])
        parts += halves(radius_ref[:, at])
        parts += [(cell // WIDE).astype(F32).astype(BF16), (cell % WIDE).astype(F32).astype(BF16)]
        a = masked(row_iota == high.astype(F32).astype(BF16), parts)
        b = marks(col_iota == low.astype(F32).astype(BF16))
        acc_ref[...] += dot(a, b, NT)
        return carry

    lax.fori_loop(0, count // STEP, place, 0)

    def pair(n):
        return acc_ref[2 * n * ROWS : (2 * n + 1) * ROWS, :], acc_ref[(2 * n + 1) * ROWS : (2 * n + 2) * ROWS, :]

    for n in range(5):
        first, second = pair(n)
        value = first + second if n < 4 else first * float(WIDE) + second
        send_ref[0:ROWS, n, :] = value[:, :SLOTS]
        send_ref[ROWS:, n, :] = value[:, SLOTS:]

    for copy in arrivals[4:]:
        copy.wait()
    cx, cy, cz = fluid_ref.shape[1:]
    for n in range(3):
        for x in range(cx):
            y_out_ref[0, n, x : x + 1, :] = fluid_ref[n, x, 0:1, :]
            y_out_ref[1, n, x : x + 1, :] = fluid_ref[n, x, cy - 1 : cy, :]

    pl.semaphore_wait(barrier, peers - 1)

    x_next, x_last = ((i + 1) % n_xs, j), ((i + n_xs - 1) % n_xs, j)
    y_next, y_last = (i, (j + 1) % n_ls), (i, (j + n_ls - 1) % n_ls)
    near = [
        pltpu.make_async_remote_copy(
            src_ref=source, dst_ref=target, send_sem=near_send.at[n], recv_sem=near_recv.at[n],
            device_id=device, device_id_type=MESH,
        )
        for n, (source, target, device) in enumerate(
            (
                (position_ref, ghost_ref, y_next),
                (radius_ref, ghost_radius_ref, y_next),
                (fluid_ref.at[:, cx - 1], x_before_ref, x_next),
                (fluid_ref.at[:, 0], x_after_ref, x_last),
                (y_out_ref.at[1], y_before_ref, y_next),
                (y_out_ref.at[0], y_after_ref, y_last),
            )
        )
    ]
    for copy in near:
        copy.start()

    def post(k, carry):
        pi, pj = peer(k)
        pltpu.make_async_remote_copy(
            src_ref=send_ref.at[pj * n_xs + pi], dst_ref=got_ref.at[me], send_sem=out_sem, recv_sem=got_sem.at[j],
            device_id=(pi, pj), device_id_type=MESH,
        ).start()
        return carry

    pltpu.make_async_copy(send_ref.at[me], got_ref.at[me], got_sem.at[j]).start()
    lax.fori_loop(1, peers, post, 0)

    near[0].wait_recv()
    near[1].wait_recv()
    kc = partners_ref.shape[0]

    def touch(c, carry):
        at = chunk_at(c, BLOCK)
        index = partners_ref[:, at]
        ghost = index >= BLOCK
        local = jnp.where(ghost, index - BLOCK, index)

        def pick(own, other):
            a = jnp.take_along_axis(jnp.broadcast_to(own, (kc, BLOCK)), local, axis=1, mode="promise_in_bounds")
            b = jnp.take_along_axis(jnp.broadcast_to(other, (kc, BLOCK)), local, axis=1, mode="promise_in_bounds")
            return jnp.where(ghost, b, a)

        diff = [
            position_ref[n : n + 1, at] - pick(position_ref[n : n + 1, at], ghost_ref[n : n + 1, at]) for n in range(3)
        ]
        other = pick(radius_ref[:, at], ghost_radius_ref[:, at])
        dist = jnp.sqrt(diff[0] * diff[0] + diff[1] * diff[1] + diff[2] * diff[2])
        delta = jnp.maximum(radius_ref[:, at] + other - dist, 0.0)
        scale = 10.0 * delta * jnp.sqrt(delta) / jnp.maximum(dist, 0.1)
        for n in range(3):
            contact_ref[n : n + 1, at] = jnp.sum(scale * diff[n], axis=0, keepdims=True)
        return carry

    lax.fori_loop(0, count // BLOCK, touch, 0, unroll=4)

    for n in range(2, 6):
        near[n].wait_recv()
    row = lax.broadcasted_iota(jnp.int32, (cy, cz), 0)
    lane = lax.broadcasted_iota(jnp.int32, (cy, cz), 1)
    for n in range(3):
        for x in range(cx):
            u = fluid_ref[n, x]
            after = fluid_ref[n, x + 1] if x + 1 < cx else x_after_ref[n]
            before = fluid_ref[n, x - 1] if x > 0 else x_before_ref[n]
            beside = after + before
            beside = beside + jnp.where(row == cy - 1, y_after_ref[n, x : x + 1, :], pltpu.roll(u, cy - 1, 0))
            beside = beside + jnp.where(row == 0, y_before_ref[n, x : x + 1, :], pltpu.roll(u, 1, 0))
            beside = beside + jnp.where(lane == cz - 1, 0.0, pltpu.roll(u, cz - 1, 1))
            beside = beside + jnp.where(lane == 0, 0.0, pltpu.roll(u, 1, 1))
            lap_ref[n, x * cy : (x + 1) * cy, :] = beside - 6.0 * u

    per = STEP // SLOTS
    acc_ref[...] = jnp.zeros_like(acc_ref)

    def joined(ref, first, n):
        return jnp.concatenate([ref[first + s, n : n + 1, :] for s in range(per)], axis=1)

    def cells(first):
        cell = joined(got_ref, first, 4)
        high = jnp.floor(cell * (1.0 / WIDE))
        return high.astype(BF16), (cell - high * WIDE).astype(BF16)

    def collect(d, carry):
        g = (j + n_ls - d) % n_ls
        here = got_ref.at[pl.ds(g * n_xs, n_xs)]
        pltpu.make_async_copy(here, here, got_sem.at[g]).wait()

        def add(c, carry):
            first = g * n_xs + c * per
            high, low = cells(first)
            rows = [joined(got_ref, first, n) for n in range(4)]
            beta = 2.0 * rows[3]
            volume = 4.0 / 3.0 * math.pi * rows[3] * rows[3] * rows[3]
            parts = []
            for x in (beta * rows[0], beta * rows[1], beta * rows[2], beta, volume):
                parts += halves(x)
            acc_ref[...] += dot(masked(row_iota == high, parts), marks(col_iota == low), NT)
            return carry

        return lax.fori_loop(0, n_xs // per, add, carry)

    lax.fori_loop(0, n_ls, collect, 0)

    def total(n):
        first, second = pair(n)
        return first + second

    porosity = 1.0 / (1.0 + total(4))
    below = porosity + 0.1 * total(3)
    for n in range(3):
        u = fluid_ref[n].reshape(ROWS, WIDE)
        star = (porosity * u + 0.1 * lap_ref[n] + 0.1 * total(n)) / below
        star_ref[n] = star.reshape(cx, cy, cz)
        high, low = halves(star)
        table_ref[n * ROWS : (n + 1) * ROWS, :] = high
        table_ref[(3 + n) * ROWS : (4 + n) * ROWS, :] = low

    def lookup(mine, low):
        x = dot(table_ref[...], marks(col_iota == low), NN)
        found = []
        for n in range(3):
            both = x[n * ROWS : (n + 1) * ROWS] + x[(3 + n) * ROWS : (4 + n) * ROWS]
            found.append(jnp.sum(jnp.where(mine, both, 0.0), axis=0, keepdims=True))
        return found

    row_f32 = lax.broadcasted_iota(jnp.int32, (ROWS, STEP), 0).astype(F32)

    def reply(d, carry):
        g = (j + n_ls - d) % n_ls

        def look(c, carry):
            first = g * n_xs + c * per
            high, low = cells(first)
            found = lookup(row_f32 == high.astype(F32), low)
            for n in range(3):
                for s in range(per):
                    answer_ref[first + s, n : n + 1, :] = found[n][:, s * SLOTS : (s + 1) * SLOTS]
            return carry

        lax.fori_loop(0, n_xs // per, look, 0)

        def back(k, carry):
            pi = (i + k) % n_xs
            pltpu.make_async_remote_copy(
                src_ref=answer_ref.at[g * n_xs + pi], dst_ref=back_ref.at[me], send_sem=answer_sem,
                recv_sem=back_sem.at[j], device_id=(pi, g), device_id_type=MESH,
            ).start()
            return carry

        @pl.when(d > 0)
        def _():
            back(0, 0)

        @pl.when(d == 0)
        def _():
            pltpu.make_async_copy(answer_ref.at[me], back_ref.at[me], back_sem.at[j]).start()

        return lax.fori_loop(1, n_xs, back, carry)

    lax.fori_loop(0, n_ls, reply, 0)
    for g in range(n_ls):
        here = back_ref.at[pl.ds(g * n_xs, n_xs)]
        pltpu.make_async_copy(here, here, back_sem.at[g]).wait()

    for n in range(3):
        high, low = halves(jnp.concatenate([back_ref[0:ROWS, n, :], back_ref[ROWS:, n, :]], axis=1))
        table_ref[n * ROWS : (n + 1) * ROWS, :] = high
        table_ref[(3 + n) * ROWS : (4 + n) * ROWS, :] = low
    row_i32 = lax.broadcasted_iota(jnp.int32, (ROWS, STEP), 0)

    def finish(c, carry):
        at = chunk_at(c, STEP)
        high, low = spot(at)
        found = lookup(row_i32 == high, low.astype(F32).astype(BF16))
        radius = radius_ref[:, at]
        beta = 2.0 * radius
        volume = 4.0 / 3.0 * math.pi * radius * radius * radius
        for n in range(3):
            velocity = velocity_ref[n : n + 1, at]
            out_ref[n : n + 1, at] = velocity + 0.1 * (
                contact_ref[n : n + 1, at] + beta * (found[n] - velocity)
            ) / (2.65 * volume)
        return carry

    lax.fori_loop(0, count // STEP, finish, 0)

    for copy in near:
        copy.wait_send()
    gone = send_ref.at[pl.ds(0, peers - 1)]
    pltpu.make_async_copy(gone, gone, out_sem).wait()
    gone = answer_ref.at[pl.ds(0, peers - 1)]
    pltpu.make_async_copy(gone, gone, answer_sem).wait()


def shards(position, velocity, radius, partners, owner, cell, fluid):
    count = radius.shape[0]
    n_xs, n_ls = lax.axis_size("xs"), lax.axis_size("ls")
    peers = n_xs * n_ls
    cx, cy, cz = fluid.shape[1:]
    anywhere = pl.BlockSpec(memory_space=pl.ANY)
    vmem = pl.BlockSpec(memory_space=pltpu.VMEM)
    arguments = (
        owner.reshape(1, count), cell.reshape(1, count), velocity, radius.reshape(1, count), position, partners, fluid,
    )
    dma = pltpu.SemaphoreType.DMA
    return pl.pallas_call(
        functools.partial(step_kernel, n_xs, n_ls),
        out_shape=(jax.ShapeDtypeStruct(velocity.shape, F32), jax.ShapeDtypeStruct(fluid.shape, F32)),
        in_specs=[anywhere] * len(arguments),
        out_specs=(vmem, vmem),
        scratch_shapes=[pltpu.VMEM(a.shape, a.dtype) for a in arguments]
        + [
            pltpu.VMEM((1, count), jnp.int32),
            pltpu.VMEM((10 * ROWS, WIDE), F32),
            pltpu.VMEM((6 * ROWS, WIDE), BF16),
            pltpu.VMEM((3, count), F32),
            pltpu.VMEM((3, ROWS, WIDE), F32),
            pltpu.VMEM((peers, 5, SLOTS), F32),
            pltpu.VMEM((peers, 5, SLOTS), F32),
            pltpu.VMEM((peers, 3, SLOTS), F32),
            pltpu.VMEM((peers, 3, SLOTS), F32),
            pltpu.VMEM((3, count), F32),
            pltpu.VMEM((1, count), F32),
            pltpu.VMEM((3, cy, cz), F32),
            pltpu.VMEM((3, cy, cz), F32),
            pltpu.VMEM((2, 3, cx, cz), F32),
            pltpu.VMEM((3, cx, cz), F32),
            pltpu.VMEM((3, cx, cz), F32),
            dma((len(arguments),)), dma((6,)), dma((6,)), dma, dma((n_ls,)), dma, dma((n_ls,)),
        ],
        compiler_params=pltpu.CompilerParams(
            collective_id=0, has_side_effects=True, vmem_limit_bytes=62 * 1024 * 1024
        ),
        cost_estimate=pl.CostEstimate(flops=14000000000, bytes_accessed=4000000, transcendentals=0),
        name="coupling",
    )(*arguments)


def solution(mesh):
    placed = (
        P(None, ("xs", "ls")),
        P(None, ("xs", "ls")),
        P(("xs", "ls")),
        P(None, ("xs", "ls")),
        P(("xs", "ls"), None),
        P(("xs", "ls")),
        P(None, "xs", "ls", None),
    )
    return jax.shard_map(
        shards,
        mesh=mesh,
        in_specs=placed,
        out_specs=(P(None, ("xs", "ls")), P(None, "xs", "ls", None)),
        check_vma=False,
    )
```

```python
import functools
import math

import jax
import jax.numpy as jnp
from jax import lax
from jax.experimental import pallas as pl
from jax.experimental.pallas import tpu as pltpu
from jax.sharding import PartitionSpec as P

F32 = jnp.float32
BF16 = jnp.bfloat16
MESH = pl.DeviceIdType.MESH
SLOTS = 128
ROWS = 64
WIDE = 256
BLOCK = 128
STEP = 4096
GROUP = 32
NT = (((1,), (1,)), ((), ()))
NN = (((1,), (0,)), ((), ()))


def halves(x):
    high = x.astype(BF16)
    return high, (x - high.astype(F32)).astype(BF16)


def dot(a, b, dims):
    return lax.dot_general(a, b, dims, preferred_element_type=F32)


def small_iota(rows, columns):
    return lax.broadcasted_iota(jnp.int32, (rows, columns), 0).astype(F32).astype(BF16)


def masked(mine, parts):
    return jnp.concatenate([jnp.where(mine, p, jnp.zeros((), BF16)) for p in parts], axis=0)


def marks(mine):
    return jnp.where(mine, jnp.ones((), BF16), jnp.zeros((), BF16))


def chunk_at(c, size):
    return pl.ds(pl.multiple_of(c * size, size), size)


def step_kernel(
    n_xs, n_ls,
    owner_in, cell_in, velocity_in, radius_in, position_in, partners_in, fluid_in,
    out_ref, star_ref,
    owner_ref, cell_ref, velocity_ref, radius_ref, position_ref, partners_ref, fluid_ref,
    slot_ref, acc_ref, table_ref, contact_ref, lap_ref,
    send_ref, got_ref, answer_ref, back_ref,
    ghost_ref, ghost_radius_ref, x_before_ref, x_after_ref, y_out_ref, y_before_ref, y_after_ref,
    in_sem, near_send, near_recv, out_sem, got_sem, answer_sem, back_sem,
):
    i = lax.axis_index("xs")
    j = lax.axis_index("ls")
    peers = n_xs * n_ls
    groups = peers // GROUP
    me = j * n_xs + i
    my_group, my_place = me // GROUP, me % GROUP
    count = owner_ref.shape[1]

    barrier = pltpu.get_barrier_semaphore()

    def peer(k):
        other = (my_group + k // GROUP) % groups * GROUP + (my_place + k % GROUP) % GROUP
        return other, (other % n_xs, other // n_xs)

    arrivals = [
        pltpu.make_async_copy(source, target, in_sem.at[n])
        for n, (source, target) in enumerate(
            (
                (owner_in, owner_ref), (cell_in, cell_ref), (velocity_in, velocity_ref), (radius_in, radius_ref),
                (position_in, position_ref), (partners_in, partners_ref), (fluid_in, fluid_ref),
            )
        )
    ]
    for copy in arrivals:
        copy.start()

    def greet(k, carry):
        pl.semaphore_signal(barrier, inc=1, device_id=peer(k)[1], device_id_type=MESH)
        return carry

    lax.fori_loop(1, peers, greet, 0)
    for copy in arrivals[:4]:
        copy.wait()

    def slot_row(owner):
        return (owner % n_ls) * n_xs + owner // n_ls

    rank_step = 256
    upper = jnp.where(
        lax.broadcasted_iota(jnp.int32, (rank_step, rank_step), 0)
        <= lax.broadcasted_iota(jnp.int32, (rank_step, rank_step), 1),
        1.0, 0.0,
    ).astype(BF16)
    owner_iota = lax.broadcasted_iota(jnp.int32, (peers, rank_step), 0)

    def rank(c, base):
        at = chunk_at(c, rank_step)
        mine = owner_iota == owner_ref[:, at]
        upto = dot(jnp.where(mine, 1.0, 0.0).astype(BF16), upper, NN) + base
        slot = jnp.sum(jnp.where(mine, upto, 0.0), axis=0, keepdims=True)
        slot_ref[:, at] = slot.astype(jnp.int32) - 1
        return upto[:, rank_step - 1 :]

    lax.fori_loop(0, count // rank_step, rank, jnp.zeros((peers, 1), F32), unroll=16)

    row_iota = small_iota(ROWS, STEP)
    col_iota = small_iota(WIDE, STEP)
    acc_ref[...] = jnp.zeros_like(acc_ref)

    def spot(at):
        row = slot_row(owner_ref[:, at])
        return row % ROWS, slot_ref[:, at] + (row // ROWS) * SLOTS

    def place(c, carry):
        at = chunk_at(c, STEP)
        high, low = spot(at)
        cell = cell_ref[:, at]
        parts = []
        for n in range(3):
            parts += halves(velocity_ref[n : n + 1, at])
        parts += halves(radius_ref[:, at])
        parts += [(cell // WIDE).astype(F32).astype(BF16), (cell % WIDE).astype(F32).astype(BF16)]
        a = masked(row_iota == high.astype(F32).astype(BF16), parts)
        b = marks(col_iota == low.astype(F32).astype(BF16))
        acc_ref[...] += dot(a, b, NT)
        return carry

    lax.fori_loop(0, count // STEP, place, 0)

    def pair(n):
        return acc_ref[2 * n * ROWS : (2 * n + 1) * ROWS, :], acc_ref[(2 * n + 1) * ROWS : (2 * n + 2) * ROWS, :]

    for n in range(5):
        first, second = pair(n)
        value = first + second if n < 4 else first * float(WIDE) + second
        send_ref[0:ROWS, n, :] = value[:, :SLOTS]
        send_ref[ROWS:, n, :] = value[:, SLOTS:]

    for copy in arrivals[4:]:
        copy.wait()
    cx, cy, cz = fluid_ref.shape[1:]
    for n in range(3):
        for x in range(cx):
            y_out_ref[0, n, x : x + 1, :] = fluid_ref[n, x, 0:1, :]
            y_out_ref[1, n, x : x + 1, :] = fluid_ref[n, x, cy - 1 : cy, :]

    pl.semaphore_wait(barrier, peers - 1)

    x_next, x_last = ((i + 1) % n_xs, j), ((i + n_xs - 1) % n_xs, j)
    y_next, y_last = (i, (j + 1) % n_ls), (i, (j + n_ls - 1) % n_ls)
    near = [
        pltpu.make_async_remote_copy(
            src_ref=source, dst_ref=target, send_sem=near_send.at[n], recv_sem=near_recv.at[n],
            device_id=device, device_id_type=MESH,
        )
        for n, (source, target, device) in enumerate(
            (
                (position_ref, ghost_ref, y_next),
                (radius_ref, ghost_radius_ref, y_next),
                (fluid_ref.at[:, cx - 1], x_before_ref, x_next),
                (fluid_ref.at[:, 0], x_after_ref, x_last),
                (y_out_ref.at[1], y_before_ref, y_next),
                (y_out_ref.at[0], y_after_ref, y_last),
            )
        )
    ]
    for copy in near:
        copy.start()

    def post(k, carry):
        other, device = peer(k)
        pltpu.make_async_remote_copy(
            src_ref=send_ref.at[other], dst_ref=got_ref.at[me], send_sem=out_sem, recv_sem=got_sem.at[my_group],
            device_id=device, device_id_type=MESH,
        ).start()
        return carry

    pltpu.make_async_copy(send_ref.at[me], got_ref.at[me], got_sem.at[my_group]).start()
    lax.fori_loop(1, peers, post, 0)

    near[0].wait_recv()
    near[1].wait_recv()
    kc = partners_ref.shape[0]

    def touch(c, carry):
        at = chunk_at(c, BLOCK)
        index = partners_ref[:, at]
        ghost = index >= BLOCK
        local = jnp.where(ghost, index - BLOCK, index)

        def pick(own, other):
            a = jnp.take_along_axis(jnp.broadcast_to(own, (kc, BLOCK)), local, axis=1, mode="promise_in_bounds")
            b = jnp.take_along_axis(jnp.broadcast_to(other, (kc, BLOCK)), local, axis=1, mode="promise_in_bounds")
            return jnp.where(ghost, b, a)

        diff = [
            position_ref[n : n + 1, at] - pick(position_ref[n : n + 1, at], ghost_ref[n : n + 1, at]) for n in range(3)
        ]
        other = pick(radius_ref[:, at], ghost_radius_ref[:, at])
        dist = jnp.sqrt(diff[0] * diff[0] + diff[1] * diff[1] + diff[2] * diff[2])
        delta = jnp.maximum(radius_ref[:, at] + other - dist, 0.0)
        scale = 10.0 * delta * jnp.sqrt(delta) / jnp.maximum(dist, 0.1)
        for n in range(3):
            contact_ref[n : n + 1, at] = jnp.sum(scale * diff[n], axis=0, keepdims=True)
        return carry

    lax.fori_loop(0, count // BLOCK, touch, 0, unroll=16)

    for n in range(2, 6):
        near[n].wait_recv()
    row = lax.broadcasted_iota(jnp.int32, (cy, cz), 0)
    lane = lax.broadcasted_iota(jnp.int32, (cy, cz), 1)
    for n in range(3):
        for x in range(cx):
            u = fluid_ref[n, x]
            after = fluid_ref[n, x + 1] if x + 1 < cx else x_after_ref[n]
            before = fluid_ref[n, x - 1] if x > 0 else x_before_ref[n]
            beside = after + before
            beside = beside + jnp.where(row == cy - 1, y_after_ref[n, x : x + 1, :], pltpu.roll(u, cy - 1, 0))
            beside = beside + jnp.where(row == 0, y_before_ref[n, x : x + 1, :], pltpu.roll(u, 1, 0))
            beside = beside + jnp.where(lane == cz - 1, 0.0, pltpu.roll(u, cz - 1, 1))
            beside = beside + jnp.where(lane == 0, 0.0, pltpu.roll(u, 1, 1))
            lap_ref[n, x * cy : (x + 1) * cy, :] = beside - 6.0 * u

    per = STEP // SLOTS
    acc_ref[...] = jnp.zeros_like(acc_ref)

    def joined(ref, first, n):
        return jnp.concatenate([ref[first + s, n : n + 1, :] for s in range(per)], axis=1)

    def cells(first):
        cell = joined(got_ref, first, 4)
        high = jnp.floor(cell * (1.0 / WIDE))
        return high.astype(BF16), (cell - high * WIDE).astype(BF16)

    def collect(d, carry):
        g = (my_group + groups - d) % groups
        here = got_ref.at[pl.ds(g * GROUP, GROUP)]
        pltpu.make_async_copy(here, here, got_sem.at[g]).wait()

        def add(c, carry):
            first = g * GROUP + c * per
            high, low = cells(first)
            rows = [joined(got_ref, first, n) for n in range(4)]
            beta = 2.0 * rows[3]
            volume = 4.0 / 3.0 * math.pi * rows[3] * rows[3] * rows[3]
            parts = []
            for x in (beta * rows[0], beta * rows[1], beta * rows[2], beta, volume):
                parts += halves(x)
            acc_ref[...] += dot(masked(row_iota == high, parts), marks(col_iota == low), NT)
            return carry

        return lax.fori_loop(0, GROUP // per, add, carry)

    lax.fori_loop(0, groups, collect, 0)

    def total(n):
        first, second = pair(n)
        return first + second

    porosity = 1.0 / (1.0 + total(4))
    below = porosity + 0.1 * total(3)
    for n in range(3):
        u = fluid_ref[n].reshape(ROWS, WIDE)
        star = (porosity * u + 0.1 * lap_ref[n] + 0.1 * total(n)) / below
        star_ref[n] = star.reshape(cx, cy, cz)
        high, low = halves(star)
        table_ref[n * ROWS : (n + 1) * ROWS, :] = high
        table_ref[(3 + n) * ROWS : (4 + n) * ROWS, :] = low

    def lookup(mine, low):
        x = dot(table_ref[...], marks(col_iota == low), NN)
        found = []
        for n in range(3):
            both = x[n * ROWS : (n + 1) * ROWS] + x[(3 + n) * ROWS : (4 + n) * ROWS]
            found.append(jnp.sum(jnp.where(mine, both, 0.0), axis=0, keepdims=True))
        return found

    row_f32 = lax.broadcasted_iota(jnp.int32, (ROWS, STEP), 0).astype(F32)

    def reply(d, carry):
        g = (my_group + groups - d) % groups

        def look(c, carry):
            first = g * GROUP + c * per
            high, low = cells(first)
            found = lookup(row_f32 == high.astype(F32), low)
            for n in range(3):
                for s in range(per):
                    answer_ref[first + s, n : n + 1, :] = found[n][:, s * SLOTS : (s + 1) * SLOTS]
            return carry

        lax.fori_loop(0, GROUP // per, look, 0)

        def back(k, carry):
            other = g * GROUP + (my_place + k) % GROUP
            pltpu.make_async_remote_copy(
                src_ref=answer_ref.at[other], dst_ref=back_ref.at[me], send_sem=answer_sem,
                recv_sem=back_sem.at[my_group], device_id=(other % n_xs, other // n_xs), device_id_type=MESH,
            ).start()
            return carry

        @pl.when(d > 0)
        def _():
            back(0, 0)

        @pl.when(d == 0)
        def _():
            pltpu.make_async_copy(answer_ref.at[me], back_ref.at[me], back_sem.at[my_group]).start()

        return lax.fori_loop(1, GROUP, back, carry)

    lax.fori_loop(0, groups, reply, 0)
    for g in range(groups):
        here = back_ref.at[pl.ds(g * GROUP, GROUP)]
        pltpu.make_async_copy(here, here, back_sem.at[g]).wait()

    for n in range(3):
        high, low = halves(jnp.concatenate([back_ref[0:ROWS, n, :], back_ref[ROWS:, n, :]], axis=1))
        table_ref[n * ROWS : (n + 1) * ROWS, :] = high
        table_ref[(3 + n) * ROWS : (4 + n) * ROWS, :] = low
    row_i32 = lax.broadcasted_iota(jnp.int32, (ROWS, STEP), 0)

    def finish(c, carry):
        at = chunk_at(c, STEP)
        high, low = spot(at)
        found = lookup(row_i32 == high, low.astype(F32).astype(BF16))
        radius = radius_ref[:, at]
        beta = 2.0 * radius
        volume = 4.0 / 3.0 * math.pi * radius * radius * radius
        for n in range(3):
            velocity = velocity_ref[n : n + 1, at]
            out_ref[n : n + 1, at] = velocity + 0.1 * (
                contact_ref[n : n + 1, at] + beta * (found[n] - velocity)
            ) / (2.65 * volume)
        return carry

    lax.fori_loop(0, count // STEP, finish, 0)

    for copy in near:
        copy.wait_send()
    gone = send_ref.at[pl.ds(0, peers - 1)]
    pltpu.make_async_copy(gone, gone, out_sem).wait()
    gone = answer_ref.at[pl.ds(0, peers - 1)]
    pltpu.make_async_copy(gone, gone, answer_sem).wait()


def shards(position, velocity, radius, partners, owner, cell, fluid):
    count = radius.shape[0]
    n_xs, n_ls = lax.axis_size("xs"), lax.axis_size("ls")
    peers = n_xs * n_ls
    cx, cy, cz = fluid.shape[1:]
    anywhere = pl.BlockSpec(memory_space=pl.ANY)
    vmem = pl.BlockSpec(memory_space=pltpu.VMEM)
    arguments = (
        owner.reshape(1, count), cell.reshape(1, count), velocity, radius.reshape(1, count), position, partners, fluid,
    )
    dma = pltpu.SemaphoreType.DMA
    return pl.pallas_call(
        functools.partial(step_kernel, n_xs, n_ls),
        out_shape=(jax.ShapeDtypeStruct(velocity.shape, F32), jax.ShapeDtypeStruct(fluid.shape, F32)),
        in_specs=[anywhere] * len(arguments),
        out_specs=(vmem, vmem),
        scratch_shapes=[pltpu.VMEM(a.shape, a.dtype) for a in arguments]
        + [
            pltpu.VMEM((1, count), jnp.int32),
            pltpu.VMEM((10 * ROWS, WIDE), F32),
            pltpu.VMEM((6 * ROWS, WIDE), BF16),
            pltpu.VMEM((3, count), F32),
            pltpu.VMEM((3, ROWS, WIDE), F32),
            pltpu.VMEM((peers, 5, SLOTS), F32),
            pltpu.VMEM((peers, 5, SLOTS), F32),
            pltpu.VMEM((peers, 3, SLOTS), F32),
            pltpu.VMEM((peers, 3, SLOTS), F32),
            pltpu.VMEM((3, count), F32),
            pltpu.VMEM((1, count), F32),
            pltpu.VMEM((3, cy, cz), F32),
            pltpu.VMEM((3, cy, cz), F32),
            pltpu.VMEM((2, 3, cx, cz), F32),
            pltpu.VMEM((3, cx, cz), F32),
            pltpu.VMEM((3, cx, cz), F32),
            dma((len(arguments),)), dma((6,)), dma((6,)), dma, dma((peers // GROUP,)), dma, dma((peers // GROUP,)),
        ],
        compiler_params=pltpu.CompilerParams(
            collective_id=0, has_side_effects=True, vmem_limit_bytes=62 * 1024 * 1024
        ),
        cost_estimate=pl.CostEstimate(flops=14000000000, bytes_accessed=4000000, transcendentals=0),
        name="coupling",
    )(*arguments)


def solution(mesh):
    placed = (
        P(None, ("xs", "ls")),
        P(None, ("xs", "ls")),
        P(("xs", "ls")),
        P(None, ("xs", "ls")),
        P(("xs", "ls"), None),
        P(("xs", "ls")),
        P(None, "xs", "ls", None),
    )
    return jax.shard_map(
        shards,
        mesh=mesh,
        in_specs=placed,
        out_specs=(P(None, ("xs", "ls")), P(None, "xs", "ls", None)),
        check_vma=False,
    )
```

```python
import functools
import math

import jax
import jax.numpy as jnp
from jax import lax
from jax.experimental import pallas as pl
from jax.experimental.pallas import tpu as pltpu
from jax.sharding import PartitionSpec as P

F32 = jnp.float32
BF16 = jnp.bfloat16
MESH = pl.DeviceIdType.MESH
SLOTS = 128
ROWS = 64
WIDE = 256
BLOCK = 128
STEP = 4096
GROUP = 32
NT = (((1,), (1,)), ((), ()))
NN = (((1,), (0,)), ((), ()))


def halves(x):
    high = x.astype(BF16)
    return high, (x - high.astype(F32)).astype(BF16)


def dot(a, b, dims):
    return lax.dot_general(a, b, dims, preferred_element_type=F32)


def small_iota(rows, columns):
    return lax.broadcasted_iota(jnp.int32, (rows, columns), 0).astype(F32).astype(BF16)


def masked(mine, parts):
    return jnp.concatenate([jnp.where(mine, p, jnp.zeros((), BF16)) for p in parts], axis=0)


def marks(mine):
    return jnp.where(mine, jnp.ones((), BF16), jnp.zeros((), BF16))


def chunk_at(c, size):
    return pl.ds(pl.multiple_of(c * size, size), size)


def step_kernel(
    n_xs, n_ls,
    owner_in, cell_in, velocity_in, radius_in, position_in, partners_in, fluid_in,
    moved_ref, star_ref,
    owner_ref, cell_ref, velocity_ref, radius_ref, position_ref, partners_ref, fluid_ref,
    slot_ref, acc_ref, table_ref, contact_ref, lap_ref,
    send_ref, got_ref, answer_ref, back_ref,
    ghost_ref, ghost_radius_ref, x_before_ref, x_after_ref, y_out_ref, y_before_ref, y_after_ref,
    in_sem, near_send, near_recv, out_sem, got_sem, answer_sem, back_sem, ready_sem,
):
    i = lax.axis_index("xs")
    j = lax.axis_index("ls")
    peers = n_xs * n_ls
    groups = peers // GROUP
    me = j * n_xs + i
    my_group, my_place = me // GROUP, me % GROUP
    count = owner_ref.shape[1]

    barrier = pltpu.get_barrier_semaphore()

    def peer(k):
        other = (my_group + k // GROUP) % groups * GROUP + (my_place + k % GROUP) % GROUP
        return other, (other % n_xs, other // n_xs)

    arrivals = [
        pltpu.make_async_copy(source, target, in_sem.at[n])
        for n, (source, target) in enumerate(
            (
                (owner_in, owner_ref), (cell_in, cell_ref), (velocity_in, velocity_ref), (radius_in, radius_ref),
                (position_in, position_ref), (partners_in, partners_ref), (fluid_in, fluid_ref),
            )
        )
    ]
    for copy in arrivals:
        copy.start()

    def greet_xs(k, carry):
        pl.semaphore_signal(barrier, inc=1, device_id=((i + k) % n_xs, j), device_id_type=MESH)
        return carry

    def greet_ls(k, carry):
        pl.semaphore_signal(barrier, inc=1, device_id=(i, (j + k) % n_ls), device_id_type=MESH)
        return carry

    def relay_ls(k, carry):
        pl.semaphore_signal(ready_sem, inc=1, device_id=(i, (j + k) % n_ls), device_id_type=MESH)
        return carry

    lax.fori_loop(1, n_xs, greet_xs, 0)
    lax.fori_loop(1, n_ls, greet_ls, 0)
    for copy in arrivals[:4]:
        copy.wait()

    def slot_row(owner):
        return (owner % n_ls) * n_xs + owner // n_ls

    rank_step = 256
    earlier = lax.broadcasted_iota(jnp.int32, (rank_step, rank_step + SLOTS), 0)
    later = lax.broadcasted_iota(jnp.int32, (rank_step, rank_step + SLOTS), 1)
    upper = jnp.where((earlier <= later) | (later >= rank_step), 1.0, 0.0).astype(BF16)
    owner_iota = lax.broadcasted_iota(jnp.int32, (peers, rank_step), 0)
    owner_small = small_iota(peers, rank_step)

    def rank(c, base):
        at = chunk_at(c, rank_step)
        owner = owner_ref[:, at]
        counts = dot(marks(owner_small == owner.astype(F32).astype(BF16)), upper, NN)
        upto = counts[:, :rank_step] + jnp.concatenate([base] * (rank_step // SLOTS), axis=1)
        slot = jnp.sum(jnp.where(owner_iota == owner, upto, 0.0), axis=0, keepdims=True)
        slot_ref[:, at] = slot.astype(jnp.int32) - 1
        return base + counts[:, rank_step:]

    lax.fori_loop(0, count // rank_step, rank, jnp.zeros((peers, SLOTS), F32), unroll=16)

    for copy in arrivals[4:]:
        copy.wait()
    cx, cy, cz = fluid_ref.shape[1:]
    for n in range(3):
        for x in range(cx):
            y_out_ref[0, n, x : x + 1, :] = fluid_ref[n, x, 0:1, :]
            y_out_ref[1, n, x : x + 1, :] = fluid_ref[n, x, cy - 1 : cy, :]

    pl.semaphore_wait(barrier, n_xs + n_ls - 2)
    lax.fori_loop(1, n_ls, relay_ls, 0)

    x_next, x_last = ((i + 1) % n_xs, j), ((i + n_xs - 1) % n_xs, j)
    y_next, y_last = (i, (j + 1) % n_ls), (i, (j + n_ls - 1) % n_ls)
    near = [
        pltpu.make_async_remote_copy(
            src_ref=source, dst_ref=target, send_sem=near_send.at[n], recv_sem=near_recv.at[n],
            device_id=device, device_id_type=MESH,
        )
        for n, (source, target, device) in enumerate(
            (
                (position_ref, ghost_ref, y_next),
                (radius_ref, ghost_radius_ref, y_next),
                (fluid_ref.at[:, cx - 1], x_before_ref, x_next),
                (fluid_ref.at[:, 0], x_after_ref, x_last),
                (y_out_ref.at[1], y_before_ref, y_next),
                (y_out_ref.at[0], y_after_ref, y_last),
            )
        )
    ]
    for copy in near:
        copy.start()

    row_iota = small_iota(ROWS, STEP)
    col_iota = small_iota(WIDE, STEP)
    acc_ref[...] = jnp.zeros_like(acc_ref)

    def spot(at):
        row = slot_row(owner_ref[:, at])
        return row % ROWS, slot_ref[:, at] + (row // ROWS) * SLOTS

    def place(c, carry):
        at = chunk_at(c, STEP)
        high, low = spot(at)
        cell = cell_ref[:, at]
        parts = []
        for n in range(3):
            parts += halves(velocity_ref[n : n + 1, at])
        parts += halves(radius_ref[:, at])
        parts += [(cell // WIDE).astype(F32).astype(BF16), (cell % WIDE).astype(F32).astype(BF16)]
        a = masked(row_iota == high.astype(F32).astype(BF16), parts)
        b = marks(col_iota == low.astype(F32).astype(BF16))
        acc_ref[...] += dot(a, b, NT)
        return carry

    lax.fori_loop(0, count // STEP, place, 0)

    def pair(n):
        return acc_ref[2 * n * ROWS : (2 * n + 1) * ROWS, :], acc_ref[(2 * n + 1) * ROWS : (2 * n + 2) * ROWS, :]

    for n in range(5):
        first, second = pair(n)
        value = first + second if n < 4 else first * float(WIDE) + second
        send_ref[0:ROWS, n, :] = value[:, :SLOTS]
        send_ref[ROWS:, n, :] = value[:, SLOTS:]

    pl.semaphore_wait(ready_sem, n_ls - 1)

    def post(k, carry):
        other, device = peer(k)
        pltpu.make_async_remote_copy(
            src_ref=send_ref.at[other], dst_ref=got_ref.at[me], send_sem=out_sem, recv_sem=got_sem.at[my_group],
            device_id=device, device_id_type=MESH,
        ).start()
        return carry

    pltpu.make_async_copy(send_ref.at[me], got_ref.at[me], got_sem.at[my_group]).start()
    lax.fori_loop(1, peers, post, 0, unroll=16)

    for n in range(2, 6):
        near[n].wait_recv()
    row = lax.broadcasted_iota(jnp.int32, (cy, cz), 0)
    lane = lax.broadcasted_iota(jnp.int32, (cy, cz), 1)
    for n in range(3):
        for x in range(cx):
            u = fluid_ref[n, x]
            after = fluid_ref[n, x + 1] if x + 1 < cx else x_after_ref[n]
            before = fluid_ref[n, x - 1] if x > 0 else x_before_ref[n]
            beside = after + before
            beside = beside + jnp.where(row == cy - 1, y_after_ref[n, x : x + 1, :], pltpu.roll(u, cy - 1, 0))
            beside = beside + jnp.where(row == 0, y_before_ref[n, x : x + 1, :], pltpu.roll(u, 1, 0))
            beside = beside + jnp.where(lane == cz - 1, 0.0, pltpu.roll(u, cz - 1, 1))
            beside = beside + jnp.where(lane == 0, 0.0, pltpu.roll(u, 1, 1))
            lap_ref[n, x * cy : (x + 1) * cy, :] = beside - 6.0 * u

    per = STEP // SLOTS
    acc_ref[...] = jnp.zeros_like(acc_ref)

    def joined(ref, first, n):
        return jnp.concatenate([ref[first + s, n : n + 1, :] for s in range(per)], axis=1)

    def cells(first):
        cell = joined(got_ref, first, 4)
        high = jnp.floor(cell * (1.0 / WIDE))
        return high.astype(BF16), (cell - high * WIDE).astype(BF16)

    def collect(d, carry):
        g = (my_group + groups - d) % groups
        here = got_ref.at[pl.ds(g * GROUP, GROUP)]
        pltpu.make_async_copy(here, here, got_sem.at[g]).wait()

        def add(c, carry):
            first = g * GROUP + c * per
            high, low = cells(first)
            rows = [joined(got_ref, first, n) for n in range(4)]
            beta = 2.0 * rows[3]
            volume = 4.0 / 3.0 * math.pi * rows[3] * rows[3] * rows[3]
            parts = []
            for x in (beta * rows[0], beta * rows[1], beta * rows[2], beta, volume):
                parts += halves(x)
            acc_ref[...] += dot(masked(row_iota == high, parts), marks(col_iota == low), NT)
            return carry

        return lax.fori_loop(0, GROUP // per, add, carry)

    lax.fori_loop(0, groups, collect, 0)

    def total(n):
        first, second = pair(n)
        return first + second

    porosity = 1.0 / (1.0 + total(4))
    below = porosity + 0.1 * total(3)
    for n in range(3):
        u = fluid_ref[n].reshape(ROWS, WIDE)
        star = (porosity * u + 0.1 * lap_ref[n] + 0.1 * total(n)) / below
        star_ref[n] = star.reshape(cx, cy, cz)
        high, low = halves(star)
        table_ref[n * ROWS : (n + 1) * ROWS, :] = high
        table_ref[(3 + n) * ROWS : (4 + n) * ROWS, :] = low

    def lookup(mine, low):
        x = dot(table_ref[...], marks(col_iota == low), NN)
        found = []
        for n in range(3):
            both = x[n * ROWS : (n + 1) * ROWS] + x[(3 + n) * ROWS : (4 + n) * ROWS]
            found.append(jnp.sum(jnp.where(mine, both, 0.0), axis=0, keepdims=True))
        return found

    row_f32 = lax.broadcasted_iota(jnp.int32, (ROWS, STEP), 0).astype(F32)

    def reply(d, carry):
        g = (my_group + groups - d) % groups

        def look(c, carry):
            first = g * GROUP + c * per
            high, low = cells(first)
            found = lookup(row_f32 == high.astype(F32), low)
            for n in range(3):
                for s in range(per):
                    answer_ref[first + s, n : n + 1, :] = found[n][:, s * SLOTS : (s + 1) * SLOTS]
            return carry

        lax.fori_loop(0, GROUP // per, look, 0)

        def back(k, carry):
            other = g * GROUP + (my_place + k) % GROUP
            pltpu.make_async_remote_copy(
                src_ref=answer_ref.at[other], dst_ref=back_ref.at[me], send_sem=answer_sem,
                recv_sem=back_sem.at[my_group], device_id=(other % n_xs, other // n_xs), device_id_type=MESH,
            ).start()
            return carry

        @pl.when(d > 0)
        def _():
            back(0, 0)

        @pl.when(d == 0)
        def _():
            pltpu.make_async_copy(answer_ref.at[me], back_ref.at[me], back_sem.at[my_group]).start()

        return lax.fori_loop(1, GROUP, back, carry, unroll=16)

    lax.fori_loop(0, groups, reply, 0)
    near[0].wait_recv()
    near[1].wait_recv()
    kc = partners_ref.shape[0]

    def touch(c, carry):
        at = chunk_at(c, BLOCK)
        index = partners_ref[:, at]
        ghost = index >= BLOCK
        local = jnp.where(ghost, index - BLOCK, index)

        def pick(own, other):
            a = jnp.take_along_axis(jnp.broadcast_to(own, (kc, BLOCK)), local, axis=1, mode="promise_in_bounds")
            b = jnp.take_along_axis(jnp.broadcast_to(other, (kc, BLOCK)), local, axis=1, mode="promise_in_bounds")
            return jnp.where(ghost, b, a)

        diff = [
            position_ref[n : n + 1, at] - pick(position_ref[n : n + 1, at], ghost_ref[n : n + 1, at]) for n in range(3)
        ]
        other = pick(radius_ref[:, at], ghost_radius_ref[:, at])
        dist = jnp.sqrt(diff[0] * diff[0] + diff[1] * diff[1] + diff[2] * diff[2])
        delta = jnp.maximum(radius_ref[:, at] + other - dist, 0.0)
        scale = 10.0 * delta * jnp.sqrt(delta) / jnp.maximum(dist, 0.1)
        for n in range(3):
            contact_ref[n : n + 1, at] = jnp.sum(scale * diff[n], axis=0, keepdims=True)
        return carry

    lax.fori_loop(0, count // BLOCK, touch, 0, unroll=16)

    for g in range(groups):
        here = back_ref.at[pl.ds(g * GROUP, GROUP)]
        pltpu.make_async_copy(here, here, back_sem.at[g]).wait()

    for n in range(3):
        high, low = halves(jnp.concatenate([back_ref[0:ROWS, n, :], back_ref[ROWS:, n, :]], axis=1))
        table_ref[n * ROWS : (n + 1) * ROWS, :] = high
        table_ref[(3 + n) * ROWS : (4 + n) * ROWS, :] = low
    row_i32 = lax.broadcasted_iota(jnp.int32, (ROWS, STEP), 0)

    def finish(c, carry):
        at = chunk_at(c, STEP)
        high, low = spot(at)
        found = lookup(row_i32 == high, low.astype(F32).astype(BF16))
        radius = radius_ref[:, at]
        beta = 2.0 * radius
        volume = 4.0 / 3.0 * math.pi * radius * radius * radius
        for n in range(3):
            velocity = velocity_ref[n : n + 1, at]
            drag = beta * (found[n] - velocity)
            moved_ref[n : n + 1, at] = velocity + 0.1 * (contact_ref[n : n + 1, at] + drag) / (2.65 * volume)
        return carry

    lax.fori_loop(0, count // STEP, finish, 0)

    for copy in near:
        copy.wait_send()
    gone = send_ref.at[pl.ds(0, peers - 1)]
    pltpu.make_async_copy(gone, gone, out_sem).wait()
    gone = answer_ref.at[pl.ds(0, peers - 1)]
    pltpu.make_async_copy(gone, gone, answer_sem).wait()


def deliver_kernel(moved_ref, star_ref, moved_out, star_out, sem):
    copies = [
        pltpu.make_async_copy(moved_ref, moved_out, sem.at[0]),
        pltpu.make_async_copy(star_ref, star_out, sem.at[1]),
    ]
    for copy in copies:
        copy.start()
    for copy in copies:
        copy.wait()


def shards(position, velocity, radius, partners, owner, cell, fluid):
    count = radius.shape[0]
    n_xs, n_ls = lax.axis_size("xs"), lax.axis_size("ls")
    peers = n_xs * n_ls
    cx, cy, cz = fluid.shape[1:]
    anywhere = pl.BlockSpec(memory_space=pl.ANY)
    vmem = pl.BlockSpec(memory_space=pltpu.VMEM)
    arguments = (
        owner.reshape(1, count), cell.reshape(1, count), velocity, radius.reshape(1, count), position, partners, fluid,
    )
    dma = pltpu.SemaphoreType.DMA
    moved, star = pl.pallas_call(
        functools.partial(step_kernel, n_xs, n_ls),
        out_shape=(jax.ShapeDtypeStruct(velocity.shape, F32), jax.ShapeDtypeStruct(fluid.shape, F32)),
        in_specs=[anywhere] * len(arguments),
        out_specs=(vmem, vmem),
        scratch_shapes=[pltpu.VMEM(a.shape, a.dtype) for a in arguments]
        + [
            pltpu.VMEM((1, count), jnp.int32),
            pltpu.VMEM((10 * ROWS, WIDE), F32),
            pltpu.VMEM((6 * ROWS, WIDE), BF16),
            pltpu.VMEM((3, count), F32),
            pltpu.VMEM((3, ROWS, WIDE), F32),
            pltpu.VMEM((peers, 5, SLOTS), F32),
            pltpu.VMEM((peers, 5, SLOTS), F32),
            pltpu.VMEM((peers, 3, SLOTS), F32),
            pltpu.VMEM((peers, 3, SLOTS), F32),
            pltpu.VMEM((3, count), F32),
            pltpu.VMEM((1, count), F32),
            pltpu.VMEM((3, cy, cz), F32),
            pltpu.VMEM((3, cy, cz), F32),
            pltpu.VMEM((2, 3, cx, cz), F32),
            pltpu.VMEM((3, cx, cz), F32),
            pltpu.VMEM((3, cx, cz), F32),
            dma((len(arguments),)), dma((6,)), dma((6,)), dma, dma((peers // GROUP,)), dma, dma((peers // GROUP,)),
            pltpu.SemaphoreType.REGULAR,
        ],
        compiler_params=pltpu.CompilerParams(
            collective_id=0, has_side_effects=True, vmem_limit_bytes=62 * 1024 * 1024
        ),
        cost_estimate=pl.CostEstimate(flops=14000000000, bytes_accessed=4000000, transcendentals=0),
        name="coupling",
    )(*arguments)
    return pl.pallas_call(
        deliver_kernel,
        out_shape=(jax.ShapeDtypeStruct(velocity.shape, F32), jax.ShapeDtypeStruct(fluid.shape, F32)),
        in_specs=[vmem, vmem],
        out_specs=(anywhere, anywhere),
        scratch_shapes=[dma((2,))],
        name="deliver",
    )(moved, star)


def solution(mesh):
    placed = (
        P(None, ("xs", "ls")),
        P(None, ("xs", "ls")),
        P(("xs", "ls")),
        P(None, ("xs", "ls")),
        P(("xs", "ls"), None),
        P(("xs", "ls")),
        P(None, "xs", "ls", None),
    )
    return jax.shard_map(
        shards,
        mesh=mesh,
        in_specs=placed,
        out_specs=(P(None, ("xs", "ls")), P(None, "xs", "ls", None)),
        check_vma=False,
    )
```

```python
import functools
import math

import jax
import jax.numpy as jnp
from jax import lax
from jax.experimental import pallas as pl
from jax.experimental.pallas import tpu as pltpu
from jax.sharding import PartitionSpec as P

F32 = jnp.float32
BF16 = jnp.bfloat16
MESH = pl.DeviceIdType.MESH
SLOTS = 128
ROWS = 64
WIDE = 256
BLOCK = 128
STEP = 4096
GROUP = 32
HALF = ROWS // 2
NT = (((1,), (1,)), ((), ()))
NN = (((1,), (0,)), ((), ()))


def halves(x):
    high = x.astype(BF16)
    return high, (x - high.astype(F32)).astype(BF16)


def dot(a, b, dims):
    return lax.dot_general(a, b, dims, preferred_element_type=F32)


def small_iota(rows, columns):
    return lax.broadcasted_iota(jnp.int32, (rows, columns), 0).astype(F32).astype(BF16)


def masked(mine, parts):
    return jnp.concatenate([jnp.where(mine, p, jnp.zeros((), BF16)) for p in parts], axis=0)


def marks(mine):
    return jnp.where(mine, jnp.ones((), BF16), jnp.zeros((), BF16))


def chunk_at(c, size):
    return pl.ds(pl.multiple_of(c * size, size), size)


def step_kernel(
    n_xs, n_ls,
    owner_in, cell_in, velocity_in, radius_in, position_in, partners_in, fluid_in,
    moved_ref, star_ref,
    owner_ref, cell_ref, velocity_ref, radius_ref, position_ref, partners_ref, fluid_ref,
    slot_ref, acc_ref, table_ref, contact_ref, seen_ref, lap_ref,
    send_ref, got_ref, answer_ref, back_ref,
    ghost_ref, ghost_radius_ref, x_before_ref, x_after_ref, y_out_ref, y_before_ref, y_after_ref,
    in_sem, near_send, near_recv, out_sem, got_sem, answer_sem, back_sem, ready_sem,
):
    i = lax.axis_index("xs")
    j = lax.axis_index("ls")
    peers = n_xs * n_ls
    groups = peers // GROUP
    me = j * n_xs + i
    my_group, my_place = me // GROUP, me % GROUP
    count = owner_ref.shape[1]

    barrier = pltpu.get_barrier_semaphore()

    arrivals = [
        pltpu.make_async_copy(source, target, in_sem.at[n])
        for n, (source, target) in enumerate(
            (
                (owner_in, owner_ref), (cell_in, cell_ref), (velocity_in, velocity_ref), (radius_in, radius_ref),
                (position_in, position_ref), (partners_in, partners_ref), (fluid_in, fluid_ref),
            )
        )
    ]
    for copy in arrivals:
        copy.start()

    def greet_xs(k, carry):
        pl.semaphore_signal(barrier, inc=1, device_id=((i + k) % n_xs, j), device_id_type=MESH)
        return carry

    def greet_ls(k, carry):
        pl.semaphore_signal(barrier, inc=1, device_id=(i, (j + k) % n_ls), device_id_type=MESH)
        return carry

    def relay_ls(k, carry):
        pl.semaphore_signal(ready_sem, inc=1, device_id=(i, (j + k) % n_ls), device_id_type=MESH)
        return carry

    lax.fori_loop(1, n_xs, greet_xs, 0)
    lax.fori_loop(1, n_ls, greet_ls, 0)
    for copy in arrivals[:4]:
        copy.wait()

    def slot_row(owner):
        return (owner % n_ls) * n_xs + owner // n_ls

    rank_step = 256
    earlier = lax.broadcasted_iota(jnp.int32, (rank_step, rank_step + SLOTS), 0)
    later = lax.broadcasted_iota(jnp.int32, (rank_step, rank_step + SLOTS), 1)
    upper = jnp.where((earlier <= later) | (later >= rank_step), 1.0, 0.0).astype(BF16)
    owner_iota = lax.broadcasted_iota(jnp.int32, (peers, rank_step), 0)
    owner_small = small_iota(peers, rank_step)

    def rank(c, base):
        at = chunk_at(c, rank_step)
        owner = owner_ref[:, at]
        counts = dot(marks(owner_small == owner.astype(F32).astype(BF16)), upper, NN)
        upto = counts[:, :rank_step] + jnp.concatenate([base] * (rank_step // SLOTS), axis=1)
        slot = jnp.sum(jnp.where(owner_iota == owner, upto, 0.0), axis=0, keepdims=True)
        slot_ref[:, at] = slot.astype(jnp.int32) - 1
        return base + counts[:, rank_step:]

    lax.fori_loop(0, count // rank_step, rank, jnp.zeros((peers, SLOTS), F32), unroll=16)

    for copy in arrivals[4:]:
        copy.wait()
    cx, cy, cz = fluid_ref.shape[1:]
    for n in range(3):
        for x in range(cx):
            y_out_ref[0, n, x : x + 1, :] = fluid_ref[n, x, 0:1, :]
            y_out_ref[1, n, x : x + 1, :] = fluid_ref[n, x, cy - 1 : cy, :]

    pl.semaphore_wait(barrier, n_xs + n_ls - 2)
    lax.fori_loop(1, n_ls, relay_ls, 0)

    x_next, x_last = ((i + 1) % n_xs, j), ((i + n_xs - 1) % n_xs, j)
    y_next, y_last = (i, (j + 1) % n_ls), (i, (j + n_ls - 1) % n_ls)
    near = [
        pltpu.make_async_remote_copy(
            src_ref=source, dst_ref=target, send_sem=near_send.at[n], recv_sem=near_recv.at[n],
            device_id=device, device_id_type=MESH,
        )
        for n, (source, target, device) in enumerate(
            (
                (position_ref, ghost_ref, y_next),
                (radius_ref, ghost_radius_ref, y_next),
                (fluid_ref.at[:, cx - 1], x_before_ref, x_next),
                (fluid_ref.at[:, 0], x_after_ref, x_last),
                (y_out_ref.at[1], y_before_ref, y_next),
                (y_out_ref.at[0], y_after_ref, y_last),
            )
        )
    ]
    for copy in near:
        copy.start()

    half_iota = small_iota(HALF, STEP)
    row_iota = small_iota(ROWS, STEP)
    col_iota = small_iota(WIDE, STEP)

    def spot(at):
        ahead = (slot_row(owner_ref[:, at]) + (groups - my_group) * GROUP) % peers
        high = ahead // (2 * GROUP) * HALF + ahead % GROUP
        low = slot_ref[:, at] + ahead // GROUP % 2 * SLOTS
        return high, low.astype(F32).astype(BF16)

    def place():
        total = jnp.zeros((10 * ROWS, WIDE), F32)
        for c in range(count // STEP):
            at = pl.ds(c * STEP, STEP)
            high, low = spot(at)
            cell = cell_ref[:, at]
            parts = []
            for n in range(3):
                parts += halves(velocity_ref[n : n + 1, at])
            parts += halves(radius_ref[:, at])
            parts += [(cell // WIDE).astype(F32).astype(BF16), (cell % WIDE).astype(F32).astype(BF16)]
            a = masked(row_iota == high.astype(F32).astype(BF16), parts)
            total = total + dot(a, marks(col_iota == low), NT)
        for n in range(5):
            first = total[2 * n * ROWS : (2 * n + 1) * ROWS]
            second = total[(2 * n + 1) * ROWS : (2 * n + 2) * ROWS]
            value = first + second if n < 4 else first * float(WIDE) + second
            send_ref[0:GROUP, n, :] = value[:HALF, :SLOTS]
            send_ref[GROUP : 2 * GROUP, n, :] = value[:HALF, SLOTS:]
            send_ref[2 * GROUP : 3 * GROUP, n, :] = value[HALF:, :SLOTS]
            send_ref[3 * GROUP :, n, :] = value[HALF:, SLOTS:]

    def post(half):
        def one(k, carry):
            place_there = (my_place + k % GROUP) % GROUP
            other = (my_group + k // GROUP) % groups * GROUP + place_there
            pltpu.make_async_remote_copy(
                src_ref=send_ref.at[k // GROUP * GROUP + place_there], dst_ref=got_ref.at[me],
                send_sem=out_sem, recv_sem=got_sem.at[my_group],
                device_id=(other % n_xs, other // n_xs), device_id_type=MESH,
            ).start()
            return carry

        if half == 0:
            pltpu.make_async_copy(send_ref.at[my_place], got_ref.at[me], got_sem.at[my_group]).start()
        first = 1 if half == 0 else 0
        lax.fori_loop(half * 2 * GROUP + first, (half + 1) * 2 * GROUP, one, 0, unroll=2 * GROUP - first)

    def pair(n):
        return acc_ref[2 * n * ROWS : (2 * n + 1) * ROWS, :], acc_ref[(2 * n + 1) * ROWS : (2 * n + 2) * ROWS, :]

    place()
    pl.semaphore_wait(ready_sem, n_ls - 1)
    post(0)
    for n in range(2, 6):
        near[n].wait_recv()
    post(1)

    row = lax.broadcasted_iota(jnp.int32, (cy, cz), 0)
    lane = lax.broadcasted_iota(jnp.int32, (cy, cz), 1)
    for n in range(3):
        for x in range(cx):
            u = fluid_ref[n, x]
            after = fluid_ref[n, x + 1] if x + 1 < cx else x_after_ref[n]
            before = fluid_ref[n, x - 1] if x > 0 else x_before_ref[n]
            beside = after + before
            beside = beside + jnp.where(row == cy - 1, y_after_ref[n, x : x + 1, :], pltpu.roll(u, cy - 1, 0))
            beside = beside + jnp.where(row == 0, y_before_ref[n, x : x + 1, :], pltpu.roll(u, 1, 0))
            beside = beside + jnp.where(lane == cz - 1, 0.0, pltpu.roll(u, cz - 1, 1))
            beside = beside + jnp.where(lane == 0, 0.0, pltpu.roll(u, 1, 1))
            lap_ref[n, x * cy : (x + 1) * cy, :] = beside - 6.0 * u

    per = STEP // SLOTS
    acc_ref[...] = jnp.zeros_like(acc_ref)

    def joined(ref, first, n):
        return jnp.concatenate([ref[first + s, n : n + 1, :] for s in range(per)], axis=1)

    def cells(first):
        cell = joined(got_ref, first, 4)
        high = jnp.floor(cell * (1.0 / WIDE))
        return high.astype(BF16), (cell - high * WIDE).astype(BF16)

    def collect(d, carry):
        g = (my_group + groups - d) % groups
        here = got_ref.at[pl.ds(g * GROUP, GROUP)]
        pltpu.make_async_copy(here, here, got_sem.at[g]).wait()

        def add(c, carry):
            first = g * GROUP + c * per
            high, low = cells(first)
            rows = [joined(got_ref, first, n) for n in range(4)]
            beta = 2.0 * rows[3]
            volume = 4.0 / 3.0 * math.pi * rows[3] * rows[3] * rows[3]
            parts = []
            for x in (beta * rows[0], beta * rows[1], beta * rows[2], beta, volume):
                parts += halves(x)
            acc_ref[...] += dot(masked(row_iota == high, parts), marks(col_iota == low), NT)
            return carry

        return lax.fori_loop(0, GROUP // per, add, carry)

    lax.fori_loop(0, groups, collect, 0)

    def total(n):
        first, second = pair(n)
        return first + second

    porosity = 1.0 / (1.0 + total(4))
    below = porosity + 0.1 * total(3)
    for n in range(3):
        u = fluid_ref[n].reshape(ROWS, WIDE)
        star = (porosity * u + 0.1 * lap_ref[n] + 0.1 * total(n)) / below
        star_ref[n] = star.reshape(cx, cy, cz)
        high, low = halves(star)
        table_ref[n * ROWS : (n + 1) * ROWS, :] = high
        table_ref[(3 + n) * ROWS : (4 + n) * ROWS, :] = low

    def lookup(rows, mine, low):
        x = dot(table_ref[0 : 6 * rows, :], marks(col_iota == low), NN)
        found = []
        for n in range(3):
            both = x[n * rows : (n + 1) * rows] + x[(3 + n) * rows : (4 + n) * rows]
            found.append(jnp.sum(jnp.where(mine, both, 0.0), axis=0, keepdims=True))
        return found

    row_f32 = lax.broadcasted_iota(jnp.int32, (ROWS, STEP), 0).astype(F32)

    def reply(d):
        group = (my_group + groups - d) % groups

        def back(k, carry):
            other = group * GROUP + (my_place + k) % GROUP
            pltpu.make_async_remote_copy(
                src_ref=answer_ref.at[other], dst_ref=back_ref.at[me], send_sem=answer_sem,
                recv_sem=back_sem.at[my_group], device_id=(other % n_xs, other // n_xs), device_id_type=MESH,
            ).start()
            return carry

        if d == 0:
            pltpu.make_async_copy(answer_ref.at[me], back_ref.at[me], back_sem.at[my_group]).start()
        first = 1 if d == 0 else 0
        lax.fori_loop(first, GROUP, back, 0, unroll=GROUP - first)

    def look(d):
        first = (my_group + groups - d) % groups * GROUP
        high, low = cells(first)
        found = lookup(ROWS, row_f32 == high.astype(F32), low)
        for n in range(3):
            for s in range(per):
                answer_ref[first + s, n : n + 1, :] = found[n][:, s * SLOTS : (s + 1) * SLOTS]

    for d in range(groups):
        if d > 0:
            reply(d - 1)
        look(d)
    reply(groups - 1)

    near[0].wait_recv()
    near[1].wait_recv()
    kc = partners_ref.shape[0]

    def touch(c, carry):
        at = chunk_at(c, BLOCK)
        index = partners_ref[:, at]
        ghost = index >= BLOCK
        local = jnp.where(ghost, index - BLOCK, index)

        def pick(own, other):
            a = jnp.take_along_axis(jnp.broadcast_to(own, (kc, BLOCK)), local, axis=1, mode="promise_in_bounds")
            b = jnp.take_along_axis(jnp.broadcast_to(other, (kc, BLOCK)), local, axis=1, mode="promise_in_bounds")
            return jnp.where(ghost, b, a)

        diff = [
            position_ref[n : n + 1, at] - pick(position_ref[n : n + 1, at], ghost_ref[n : n + 1, at]) for n in range(3)
        ]
        other = pick(radius_ref[:, at], ghost_radius_ref[:, at])
        dist = jnp.sqrt(diff[0] * diff[0] + diff[1] * diff[1] + diff[2] * diff[2])
        delta = jnp.maximum(radius_ref[:, at] + other - dist, 0.0)
        scale = 10.0 * delta * jnp.sqrt(delta) / jnp.maximum(dist, 0.1)
        for n in range(3):
            contact_ref[n : n + 1, at] = jnp.sum(scale * diff[n], axis=0, keepdims=True)
        return carry

    lax.fori_loop(0, count // BLOCK, touch, 0, unroll=16)

    row_i32 = lax.broadcasted_iota(jnp.int32, (HALF, STEP), 0)
    for half in range(2):
        starts = []
        for d in (2 * half, 2 * half + 1):
            group = (my_group + d) % groups
            here = back_ref.at[pl.ds(group * GROUP, GROUP)]
            pltpu.make_async_copy(here, here, back_sem.at[group]).wait()
            starts.append(group * GROUP)
        for n in range(3):
            both = jnp.concatenate([back_ref[pl.ds(start, GROUP), n, :] for start in starts], axis=1)
            high, low = halves(both)
            table_ref[n * HALF : (n + 1) * HALF, :] = high
            table_ref[(3 + n) * HALF : (4 + n) * HALF, :] = low

        for c in range(count // STEP):
            at = pl.ds(c * STEP, STEP)
            high, low = spot(at)
            found = lookup(HALF, row_i32 == high - half * HALF, low)
            if half == 0:
                for n in range(3):
                    seen_ref[n : n + 1, at] = found[n]
                continue
            radius = radius_ref[:, at]
            beta = 2.0 * radius
            volume = 4.0 / 3.0 * math.pi * radius * radius * radius
            for n in range(3):
                velocity = velocity_ref[n : n + 1, at]
                drag = beta * (seen_ref[n : n + 1, at] + found[n] - velocity)
                moved_ref[n : n + 1, at] = velocity + 0.1 * (contact_ref[n : n + 1, at] + drag) / (2.65 * volume)

    for copy in near:
        copy.wait_send()
    gone = send_ref.at[pl.ds(0, peers - 1)]
    pltpu.make_async_copy(gone, gone, out_sem).wait()
    gone = answer_ref.at[pl.ds(0, peers - 1)]
    pltpu.make_async_copy(gone, gone, answer_sem).wait()


def deliver_kernel(moved_ref, star_ref, moved_out, star_out, sem):
    copies = [
        pltpu.make_async_copy(moved_ref, moved_out, sem.at[0]),
        pltpu.make_async_copy(star_ref, star_out, sem.at[1]),
    ]
    for copy in copies:
        copy.start()
    for copy in copies:
        copy.wait()


def shards(position, velocity, radius, partners, owner, cell, fluid):
    count = radius.shape[0]
    n_xs, n_ls = lax.axis_size("xs"), lax.axis_size("ls")
    peers = n_xs * n_ls
    cx, cy, cz = fluid.shape[1:]
    anywhere = pl.BlockSpec(memory_space=pl.ANY)
    vmem = pl.BlockSpec(memory_space=pltpu.VMEM)
    arguments = (
        owner.reshape(1, count), cell.reshape(1, count), velocity, radius.reshape(1, count), position, partners, fluid,
    )
    dma = pltpu.SemaphoreType.DMA
    moved, star = pl.pallas_call(
        functools.partial(step_kernel, n_xs, n_ls),
        out_shape=(jax.ShapeDtypeStruct(velocity.shape, F32), jax.ShapeDtypeStruct(fluid.shape, F32)),
        in_specs=[anywhere] * len(arguments),
        out_specs=(vmem, vmem),
        scratch_shapes=[pltpu.VMEM(a.shape, a.dtype) for a in arguments]
        + [
            pltpu.VMEM((1, count), jnp.int32),
            pltpu.VMEM((10 * ROWS, WIDE), F32),
            pltpu.VMEM((6 * ROWS, WIDE), BF16),
            pltpu.VMEM((3, count), F32),
            pltpu.VMEM((3, count), F32),
            pltpu.VMEM((3, ROWS, WIDE), F32),
            pltpu.VMEM((peers, 5, SLOTS), F32),
            pltpu.VMEM((peers, 5, SLOTS), F32),
            pltpu.VMEM((peers, 3, SLOTS), F32),
            pltpu.VMEM((peers, 3, SLOTS), F32),
            pltpu.VMEM((3, count), F32),
            pltpu.VMEM((1, count), F32),
            pltpu.VMEM((3, cy, cz), F32),
            pltpu.VMEM((3, cy, cz), F32),
            pltpu.VMEM((2, 3, cx, cz), F32),
            pltpu.VMEM((3, cx, cz), F32),
            pltpu.VMEM((3, cx, cz), F32),
            dma((len(arguments),)), dma((6,)), dma((6,)), dma, dma((peers // GROUP,)), dma, dma((peers // GROUP,)),
            pltpu.SemaphoreType.REGULAR,
        ],
        compiler_params=pltpu.CompilerParams(
            collective_id=0, has_side_effects=True, vmem_limit_bytes=62 * 1024 * 1024
        ),
        cost_estimate=pl.CostEstimate(flops=14000000000, bytes_accessed=4000000, transcendentals=0),
        name="coupling",
    )(*arguments)
    return pl.pallas_call(
        deliver_kernel,
        out_shape=(jax.ShapeDtypeStruct(velocity.shape, F32), jax.ShapeDtypeStruct(fluid.shape, F32)),
        in_specs=[vmem, vmem],
        out_specs=(anywhere, anywhere),
        scratch_shapes=[dma((2,))],
        name="deliver",
    )(moved, star)


def solution(mesh):
    placed = (
        P(None, ("xs", "ls")),
        P(None, ("xs", "ls")),
        P(("xs", "ls")),
        P(None, ("xs", "ls")),
        P(("xs", "ls"), None),
        P(("xs", "ls")),
        P(None, "xs", "ls", None),
    )
    return jax.shard_map(
        shards,
        mesh=mesh,
        in_specs=placed,
        out_specs=(P(None, ("xs", "ls")), P(None, "xs", "ls", None)),
        check_vma=False,
    )
```

```python
import functools
import math

import jax
import jax.numpy as jnp
from jax import lax
from jax.experimental import pallas as pl
from jax.experimental.pallas import tpu as pltpu
from jax.sharding import PartitionSpec as P

F32 = jnp.float32
BF16 = jnp.bfloat16
MESH = pl.DeviceIdType.MESH
SLOTS = 128
ROWS = 64
WIDE = 256
BLOCK = 128
STEP = 4096
GROUP = 32
HALF = ROWS // 2
NT = (((1,), (1,)), ((), ()))
NN = (((1,), (0,)), ((), ()))


def halves(x):
    high = x.astype(BF16)
    return high, (x - high.astype(F32)).astype(BF16)


def dot(a, b, dims):
    return lax.dot_general(a, b, dims, preferred_element_type=F32)


def small_iota(rows, columns):
    return lax.broadcasted_iota(jnp.int32, (rows, columns), 0).astype(F32).astype(BF16)


def masked(mine, parts):
    return jnp.concatenate([jnp.where(mine, p, jnp.zeros((), BF16)) for p in parts], axis=0)


def marks(mine):
    return jnp.where(mine, jnp.ones((), BF16), jnp.zeros((), BF16))


def chunk_at(c, size):
    return pl.ds(pl.multiple_of(c * size, size), size)


def step_kernel(
    n_xs, n_ls,
    owner_in, cell_in, velocity_in, radius_in, position_in, partners_in, fluid_in,
    moved_ref, star_ref,
    owner_ref, cell_ref, velocity_ref, radius_ref, position_ref, partners_ref, fluid_ref,
    slot_ref, acc_ref, table_ref, contact_ref, seen_ref, lap_ref,
    send_ref, got_ref, answer_ref, back_ref,
    ghost_ref, ghost_radius_ref, x_before_ref, x_after_ref, y_out_ref, y_before_ref, y_after_ref,
    in_sem, near_send, near_recv, out_sem, got_sem, answer_sem, back_sem, ready_sem,
):
    i = lax.axis_index("xs")
    j = lax.axis_index("ls")
    peers = n_xs * n_ls
    groups = peers // GROUP
    me = j * n_xs + i
    my_group, my_place = me // GROUP, me % GROUP
    count = owner_ref.shape[1]

    barrier = pltpu.get_barrier_semaphore()

    arrivals = [
        pltpu.make_async_copy(source, target, in_sem.at[n])
        for n, (source, target) in enumerate(
            (
                (owner_in, owner_ref), (cell_in, cell_ref), (velocity_in, velocity_ref), (radius_in, radius_ref),
                (position_in, position_ref), (partners_in, partners_ref), (fluid_in, fluid_ref),
            )
        )
    ]
    for copy in arrivals:
        copy.start()

    def greet_xs(k, carry):
        pl.semaphore_signal(barrier, inc=1, device_id=((i + k) % n_xs, j), device_id_type=MESH)
        return carry

    def greet_ls(k, carry):
        pl.semaphore_signal(barrier, inc=1, device_id=(i, (j + k) % n_ls), device_id_type=MESH)
        return carry

    def relay_ls(k, carry):
        pl.semaphore_signal(ready_sem, inc=1, device_id=(i, (j + k) % n_ls), device_id_type=MESH)
        return carry

    lax.fori_loop(1, n_xs, greet_xs, 0)
    lax.fori_loop(1, n_ls, greet_ls, 0)
    for copy in arrivals[:4]:
        copy.wait()

    def slot_row(owner):
        return (owner % n_ls) * n_xs + owner // n_ls

    rank_step = 256
    earlier = lax.broadcasted_iota(jnp.int32, (rank_step, rank_step + SLOTS), 0)
    later = lax.broadcasted_iota(jnp.int32, (rank_step, rank_step + SLOTS), 1)
    upper = jnp.where((earlier <= later) | (later >= rank_step), 1.0, 0.0).astype(BF16)
    owner_iota = lax.broadcasted_iota(jnp.int32, (peers, rank_step), 0)
    owner_small = small_iota(peers, rank_step)

    def rank(c, base):
        at = chunk_at(c, rank_step)
        owner = owner_ref[:, at]
        counts = dot(marks(owner_small == owner.astype(F32).astype(BF16)), upper, NN)
        upto = counts[:, :rank_step] + jnp.concatenate([base] * (rank_step // SLOTS), axis=1)
        slot = jnp.sum(jnp.where(owner_iota == owner, upto, 0.0), axis=0, keepdims=True)
        slot_ref[:, at] = slot.astype(jnp.int32) - 1
        return base + counts[:, rank_step:]

    lax.fori_loop(0, count // rank_step, rank, jnp.zeros((peers, SLOTS), F32), unroll=16)

    for copy in arrivals[4:]:
        copy.wait()
    cx, cy, cz = fluid_ref.shape[1:]
    for n in range(3):
        for x in range(cx):
            y_out_ref[0, n, x : x + 1, :] = fluid_ref[n, x, 0:1, :]
            y_out_ref[1, n, x : x + 1, :] = fluid_ref[n, x, cy - 1 : cy, :]

    pl.semaphore_wait(barrier, n_xs + n_ls - 2)
    lax.fori_loop(1, n_ls, relay_ls, 0)

    x_next, x_last = ((i + 1) % n_xs, j), ((i + n_xs - 1) % n_xs, j)
    y_next, y_last = (i, (j + 1) % n_ls), (i, (j + n_ls - 1) % n_ls)
    near = [
        pltpu.make_async_remote_copy(
            src_ref=source, dst_ref=target, send_sem=near_send.at[n], recv_sem=near_recv.at[n],
            device_id=device, device_id_type=MESH,
        )
        for n, (source, target, device) in enumerate(
            (
                (position_ref, ghost_ref, y_next),
                (radius_ref, ghost_radius_ref, y_next),
                (fluid_ref.at[:, cx - 1], x_before_ref, x_next),
                (fluid_ref.at[:, 0], x_after_ref, x_last),
                (y_out_ref.at[1], y_before_ref, y_next),
                (y_out_ref.at[0], y_after_ref, y_last),
            )
        )
    ]
    for copy in near:
        copy.start()

    half_iota = small_iota(HALF, STEP)
    row_iota = small_iota(ROWS, STEP)
    col_iota = small_iota(WIDE, STEP)

    def spot(at):
        ahead = (slot_row(owner_ref[:, at]) + (groups - my_group) * GROUP) % peers
        high = ahead // (2 * GROUP) * HALF + ahead % GROUP
        low = slot_ref[:, at] + ahead // GROUP % 2 * SLOTS
        return high, low.astype(F32).astype(BF16)

    def place():
        total = jnp.zeros((10 * ROWS, WIDE), F32)
        for c in range(count // STEP):
            at = pl.ds(c * STEP, STEP)
            high, low = spot(at)
            cell = cell_ref[:, at]
            parts = []
            for n in range(3):
                parts += halves(velocity_ref[n : n + 1, at])
            parts += halves(radius_ref[:, at])
            parts += [(cell // WIDE).astype(F32).astype(BF16), (cell % WIDE).astype(F32).astype(BF16)]
            a = masked(row_iota == high.astype(F32).astype(BF16), parts)
            total = total + dot(a, marks(col_iota == low), NT)
        for n in range(5):
            first = total[2 * n * ROWS : (2 * n + 1) * ROWS]
            second = total[(2 * n + 1) * ROWS : (2 * n + 2) * ROWS]
            value = first + second if n < 4 else first * float(WIDE) + second
            send_ref[0:GROUP, n, :] = value[:HALF, :SLOTS]
            send_ref[GROUP : 2 * GROUP, n, :] = value[:HALF, SLOTS:]
            send_ref[2 * GROUP : 3 * GROUP, n, :] = value[HALF:, :SLOTS]
            send_ref[3 * GROUP :, n, :] = value[HALF:, SLOTS:]

    def post(half):
        def one(k, carry):
            place_there = (my_place + k % GROUP) % GROUP
            other = (my_group + k // GROUP) % groups * GROUP + place_there
            pltpu.make_async_remote_copy(
                src_ref=send_ref.at[k // GROUP * GROUP + place_there], dst_ref=got_ref.at[me],
                send_sem=out_sem, recv_sem=got_sem.at[my_group],
                device_id=(other % n_xs, other // n_xs), device_id_type=MESH,
            ).start()
            return carry

        if half == 0:
            pltpu.make_async_copy(send_ref.at[my_place], got_ref.at[me], got_sem.at[my_group]).start()
        first = 1 if half == 0 else 0
        lax.fori_loop(half * 2 * GROUP + first, (half + 1) * 2 * GROUP, one, 0, unroll=2 * GROUP - first)

    def pair(n):
        return acc_ref[2 * n * ROWS : (2 * n + 1) * ROWS, :], acc_ref[(2 * n + 1) * ROWS : (2 * n + 2) * ROWS, :]

    place()
    pl.semaphore_wait(ready_sem, n_ls - 1)
    post(0)
    for n in range(2, 6):
        near[n].wait_recv()
    post(1)

    per = STEP // SLOTS
    acc_ref[...] = jnp.zeros_like(acc_ref)

    def joined(ref, first, n):
        return jnp.concatenate([ref[first + s, n : n + 1, :] for s in range(per)], axis=1)

    def cells(first):
        cell = joined(got_ref, first, 4)
        high = jnp.floor(cell * (1.0 / WIDE))
        return high.astype(BF16), (cell - high * WIDE).astype(BF16)

    def collect(d, carry):
        g = (my_group + groups - d) % groups
        here = got_ref.at[pl.ds(g * GROUP, GROUP)]
        pltpu.make_async_copy(here, here, got_sem.at[g]).wait()

        def add(c, carry):
            first = g * GROUP + c * per
            high, low = cells(first)
            rows = [joined(got_ref, first, n) for n in range(4)]
            beta = 2.0 * rows[3]
            volume = 4.0 / 3.0 * math.pi * rows[3] * rows[3] * rows[3]
            parts = []
            for x in (beta * rows[0], beta * rows[1], beta * rows[2], beta, volume):
                parts += halves(x)
            acc_ref[...] += dot(masked(row_iota == high, parts), marks(col_iota == low), NT)
            return carry

        return lax.fori_loop(0, GROUP // per, add, carry)

    lax.fori_loop(0, groups, collect, 0)

    def total(n):
        first, second = pair(n)
        return first + second

    row = lax.broadcasted_iota(jnp.int32, (cy, cz), 0)
    lane = lax.broadcasted_iota(jnp.int32, (cy, cz), 1)
    for n in range(3):
        for x in range(cx):
            u = fluid_ref[n, x]
            after = fluid_ref[n, x + 1] if x + 1 < cx else x_after_ref[n]
            before = fluid_ref[n, x - 1] if x > 0 else x_before_ref[n]
            beside = after + before
            beside = beside + jnp.where(row == cy - 1, y_after_ref[n, x : x + 1, :], pltpu.roll(u, cy - 1, 0))
            beside = beside + jnp.where(row == 0, y_before_ref[n, x : x + 1, :], pltpu.roll(u, 1, 0))
            beside = beside + jnp.where(lane == cz - 1, 0.0, pltpu.roll(u, cz - 1, 1))
            beside = beside + jnp.where(lane == 0, 0.0, pltpu.roll(u, 1, 1))
            lap_ref[n, x * cy : (x + 1) * cy, :] = beside - 6.0 * u

    porosity = 1.0 / (1.0 + total(4))
    below = porosity + 0.1 * total(3)
    for n in range(3):
        u = fluid_ref[n].reshape(ROWS, WIDE)
        star = (porosity * u + 0.1 * lap_ref[n] + 0.1 * total(n)) / below
        star_ref[n] = star.reshape(cx, cy, cz)
        high, low = halves(star)
        table_ref[n * ROWS : (n + 1) * ROWS, :] = high
        table_ref[(3 + n) * ROWS : (4 + n) * ROWS, :] = low

    def lookup(rows, mine, low):
        x = dot(table_ref[0 : 6 * rows, :], marks(col_iota == low), NN)
        found = []
        for n in range(3):
            both = x[n * rows : (n + 1) * rows] + x[(3 + n) * rows : (4 + n) * rows]
            found.append(jnp.sum(jnp.where(mine, both, 0.0), axis=0, keepdims=True))
        return found

    row_f32 = lax.broadcasted_iota(jnp.int32, (ROWS, STEP), 0).astype(F32)

    def reply(d):
        group = (my_group + groups - d) % groups

        def back(k, carry):
            other = group * GROUP + (my_place + k) % GROUP
            pltpu.make_async_remote_copy(
                src_ref=answer_ref.at[other], dst_ref=back_ref.at[me], send_sem=answer_sem,
                recv_sem=back_sem.at[my_group], device_id=(other % n_xs, other // n_xs), device_id_type=MESH,
            ).start()
            return carry

        if d == 0:
            pltpu.make_async_copy(answer_ref.at[me], back_ref.at[me], back_sem.at[my_group]).start()
        first = 1 if d == 0 else 0
        lax.fori_loop(first, GROUP, back, 0, unroll=GROUP - first)

    def look(d):
        first = (my_group + groups - d) % groups * GROUP
        high, low = cells(first)
        found = lookup(ROWS, row_f32 == high.astype(F32), low)
        for n in range(3):
            for s in range(per):
                answer_ref[first + s, n : n + 1, :] = found[n][:, s * SLOTS : (s + 1) * SLOTS]

    for d in range(groups):
        if d > 0:
            reply(d - 1)
        look(d)
    reply(groups - 1)

    near[0].wait_recv()
    near[1].wait_recv()
    kc = partners_ref.shape[0]

    def touch(c, carry):
        at = chunk_at(c, BLOCK)
        index = partners_ref[:, at]
        ghost = index >= BLOCK
        local = jnp.where(ghost, index - BLOCK, index)

        def pick(own, other):
            a = jnp.take_along_axis(jnp.broadcast_to(own, (kc, BLOCK)), local, axis=1, mode="promise_in_bounds")
            b = jnp.take_along_axis(jnp.broadcast_to(other, (kc, BLOCK)), local, axis=1, mode="promise_in_bounds")
            return jnp.where(ghost, b, a)

        diff = [
            position_ref[n : n + 1, at] - pick(position_ref[n : n + 1, at], ghost_ref[n : n + 1, at]) for n in range(3)
        ]
        other = pick(radius_ref[:, at], ghost_radius_ref[:, at])
        dist = jnp.sqrt(diff[0] * diff[0] + diff[1] * diff[1] + diff[2] * diff[2])
        delta = jnp.maximum(radius_ref[:, at] + other - dist, 0.0)
        scale = 10.0 * delta * jnp.sqrt(delta) / jnp.maximum(dist, 0.1)
        for n in range(3):
            contact_ref[n : n + 1, at] = jnp.sum(scale * diff[n], axis=0, keepdims=True)
        return carry

    lax.fori_loop(0, count // BLOCK, touch, 0, unroll=16)

    row_i32 = lax.broadcasted_iota(jnp.int32, (HALF, STEP), 0)
    for half in range(2):
        starts = []
        for d in (2 * half, 2 * half + 1):
            group = (my_group + d) % groups
            here = back_ref.at[pl.ds(group * GROUP, GROUP)]
            pltpu.make_async_copy(here, here, back_sem.at[group]).wait()
            starts.append(group * GROUP)
        for n in range(3):
            both = jnp.concatenate([back_ref[pl.ds(start, GROUP), n, :] for start in starts], axis=1)
            high, low = halves(both)
            table_ref[n * HALF : (n + 1) * HALF, :] = high
            table_ref[(3 + n) * HALF : (4 + n) * HALF, :] = low

        for c in range(count // STEP):
            at = pl.ds(c * STEP, STEP)
            high, low = spot(at)
            found = lookup(HALF, row_i32 == high - half * HALF, low)
            if half == 0:
                for n in range(3):
                    seen_ref[n : n + 1, at] = found[n]
                continue
            radius = radius_ref[:, at]
            beta = 2.0 * radius
            volume = 4.0 / 3.0 * math.pi * radius * radius * radius
            for n in range(3):
                velocity = velocity_ref[n : n + 1, at]
                drag = beta * (seen_ref[n : n + 1, at] + found[n] - velocity)
                moved_ref[n : n + 1, at] = velocity + 0.1 * (contact_ref[n : n + 1, at] + drag) / (2.65 * volume)

    for copy in near:
        copy.wait_send()
    gone = send_ref.at[pl.ds(0, peers - 1)]
    pltpu.make_async_copy(gone, gone, out_sem).wait()
    gone = answer_ref.at[pl.ds(0, peers - 1)]
    pltpu.make_async_copy(gone, gone, answer_sem).wait()


def deliver_kernel(moved_ref, star_ref, moved_out, star_out, sem):
    copies = [
        pltpu.make_async_copy(moved_ref, moved_out, sem.at[0]),
        pltpu.make_async_copy(star_ref, star_out, sem.at[1]),
    ]
    for copy in copies:
        copy.start()
    for copy in copies:
        copy.wait()


def shards(position, velocity, radius, partners, owner, cell, fluid):
    count = radius.shape[0]
    n_xs, n_ls = lax.axis_size("xs"), lax.axis_size("ls")
    peers = n_xs * n_ls
    cx, cy, cz = fluid.shape[1:]
    anywhere = pl.BlockSpec(memory_space=pl.ANY)
    vmem = pl.BlockSpec(memory_space=pltpu.VMEM)
    arguments = (
        owner.reshape(1, count), cell.reshape(1, count), velocity, radius.reshape(1, count), position, partners, fluid,
    )
    dma = pltpu.SemaphoreType.DMA
    moved, star = pl.pallas_call(
        functools.partial(step_kernel, n_xs, n_ls),
        out_shape=(jax.ShapeDtypeStruct(velocity.shape, F32), jax.ShapeDtypeStruct(fluid.shape, F32)),
        in_specs=[anywhere] * len(arguments),
        out_specs=(vmem, vmem),
        scratch_shapes=[pltpu.VMEM(a.shape, a.dtype) for a in arguments]
        + [
            pltpu.VMEM((1, count), jnp.int32),
            pltpu.VMEM((10 * ROWS, WIDE), F32),
            pltpu.VMEM((6 * ROWS, WIDE), BF16),
            pltpu.VMEM((3, count), F32),
            pltpu.VMEM((3, count), F32),
            pltpu.VMEM((3, ROWS, WIDE), F32),
            pltpu.VMEM((peers, 5, SLOTS), F32),
            pltpu.VMEM((peers, 5, SLOTS), F32),
            pltpu.VMEM((peers, 3, SLOTS), F32),
            pltpu.VMEM((peers, 3, SLOTS), F32),
            pltpu.VMEM((3, count), F32),
            pltpu.VMEM((1, count), F32),
            pltpu.VMEM((3, cy, cz), F32),
            pltpu.VMEM((3, cy, cz), F32),
            pltpu.VMEM((2, 3, cx, cz), F32),
            pltpu.VMEM((3, cx, cz), F32),
            pltpu.VMEM((3, cx, cz), F32),
            dma((len(arguments),)), dma((6,)), dma((6,)), dma, dma((peers // GROUP,)), dma, dma((peers // GROUP,)),
            pltpu.SemaphoreType.REGULAR,
        ],
        compiler_params=pltpu.CompilerParams(
            collective_id=0, has_side_effects=True, vmem_limit_bytes=62 * 1024 * 1024
        ),
        cost_estimate=pl.CostEstimate(flops=14000000000, bytes_accessed=4000000, transcendentals=0),
        name="coupling",
    )(*arguments)
    return pl.pallas_call(
        deliver_kernel,
        out_shape=(jax.ShapeDtypeStruct(velocity.shape, F32), jax.ShapeDtypeStruct(fluid.shape, F32)),
        in_specs=[vmem, vmem],
        out_specs=(anywhere, anywhere),
        scratch_shapes=[dma((2,))],
        name="deliver",
    )(moved, star)


def solution(mesh):
    placed = (
        P(None, ("xs", "ls")),
        P(None, ("xs", "ls")),
        P(("xs", "ls")),
        P(None, ("xs", "ls")),
        P(("xs", "ls"), None),
        P(("xs", "ls")),
        P(None, "xs", "ls", None),
    )
    return jax.shard_map(
        shards,
        mesh=mesh,
        in_specs=placed,
        out_specs=(P(None, ("xs", "ls")), P(None, "xs", "ls", None)),
        check_vma=False,
    )
```
